512 devices in a mesh: ctx: 32 (over x, y, core), exp: 16 (over z).
Axes of the slice: x: 4, y: 4, z: 16, core: 2. Of those that a mesh axis runs over, the one named last changes fastest.
Arguments:
- queries: bfloat16 [8192, 4096], P('ctx', 'exp'), may hold values from -6 to 6
- keys: bfloat16 [8192, 512], P('ctx'), may hold values from -6 to 6
- values: bfloat16 [8192, 512], P('ctx'), may hold values from -6 to 6
- out_proj: bfloat16 [4096, 2048], P('exp'), may hold values from -0.09375 to 0.09375
- resid: bfloat16 [8192, 2048], P('ctx'), may hold values from -12 to 12
- norm_gain: float32 [2048], replicated, may hold values from 0.1 to 1.9
- routes: int32 [8192, 8], P('ctx'), may hold values from 0 to 15, all different within a row; in each aligned block of 16 rows (0 to 15, 16 to 31, ...) at most 12 rows name the same one
- gates: float32 [8192, 8], P('ctx'), may hold values from 0.05 to 1
- w_gate: bfloat16 [16, 2048, 768], P('exp', 'ctx'), may hold values from -0.125 to 0.125
- w_up: bfloat16 [16, 2048, 768], P('exp', 'ctx'), may hold values from -0.125 to 0.125
- w_down: bfloat16 [16, 768, 2048], P('exp', None, 'ctx'), may hold values from -0.21875 to 0.21875
Outputs:
- attn: bfloat16 [8192, 4096], P('ctx', 'exp')
- layer_out: bfloat16 [8192, 2048], P(('ctx', 'exp'))
The draws below stay inside these ranges and needn't reach their ends.
Inputs may be any that keep to these rules, and one draw needn't show every extreme that they name: `routes`: each row names 8 different experts; in every aligned block of 16 rows no expert is named by more than 12 rows, a bound that some block reaches.
All inputs are finite; a program needn't handle non-finite values.
Results may differ from the reference program's by a relative error of at most 0.02.
Values may be sent and summed in bfloat16 or wider, within the bound.
A program may use at most 64 MiB of HBM per device.

```python
import math
import jax
import jax.numpy as jnp
import numpy as np
from jax import lax

D = 2048
FF = 768
QUERY_HEADS = 32
KEY_VALUE_HEADS = 4
HEAD_SIZE = 128
EXPERTS = 16
TOP = 8
SEQUENCE_TOKENS = 8192
MOE_TOK = 16
CAP = 12
N_CTX = 32
N_EXP = 16


def draw_queries(key, part):
    key = jax.random.fold_in(key, 11)
    base_offset = jnp.clip(1.5 * jax.random.normal(key, (SEQUENCE_TOKENS, QUERY_HEADS, HEAD_SIZE), jnp.float32), -6.0, 6.0)
    return base_offset.reshape(SEQUENCE_TOKENS, QUERY_HEADS * HEAD_SIZE).astype(jnp.bfloat16)


def draw_keys(key, part):
    key = jax.random.fold_in(key, 12)
    base_offset = jnp.clip(jax.random.normal(key, (SEQUENCE_TOKENS, KEY_VALUE_HEADS, HEAD_SIZE), jnp.float32), -6.0, 6.0)
    return base_offset.reshape(SEQUENCE_TOKENS, KEY_VALUE_HEADS * HEAD_SIZE).astype(jnp.bfloat16)


def draw_resid(key, part):
    key = jax.random.fold_in(key, 13)
    row_key, col_key, body_key = jax.random.split(key, 3)
    row_scale = jnp.exp(jax.random.uniform(row_key, (SEQUENCE_TOKENS, 1), jnp.float32, math.log(0.1), math.log(1.0)))
    col_scale = jnp.exp(jax.random.uniform(col_key, (1, D), jnp.float32, math.log(0.3), math.log(3.0)))
    base_offset = jax.random.normal(body_key, (SEQUENCE_TOKENS, D), jnp.float32)
    return jnp.clip(base_offset * row_scale * col_scale, -12.0, 12.0).astype(jnp.bfloat16)


def steps_of(stream_key, shape, cuts, low, largest):
    def one(dim, parts):
        draws = jax.random.uniform(jax.random.fold_in(jax.random.fold_in(stream_key, 6), dim), (parts,), jnp.float32, low / len(cuts), largest / len(cuts))
        return jnp.repeat(jnp.exp(draws), shape[dim] // parts).reshape((-1,) + (1,) * (len(shape) - dim - 1))

    factor_of = one(*cuts[0])
    for cut in cuts[1:]:
        factor_of = factor_of * one(*cut)
    return factor_of


def routed_block(key, own, number, rows, count, top, limit, slope):
    ranking = jax.random.permutation(key, count)
    crowded, usual = portions_of(count, rows * top, limit, slope, True), portions_of(count, rows * top, limit, slope, False)
    places = jnp.arange(count)

    def named(lengths, turn):
        used = int((lengths > 0).sum())
        fixed = max(1, used // 4)
        shifted = fixed + (places - fixed + turn * (used - fixed)) % max(1, count - fixed)
        return jnp.zeros((count,), jnp.int32).at[ranking[jnp.where(places < fixed, places, shifted)]].set(jnp.asarray(lengths, jnp.int32))

    lengths = jnp.where(number % 4 == 0, named(crowded, number // 4), named(usual, number - number // 4 - 1))
    mixed = jax.random.permutation(jax.random.fold_in(own, 3), count)
    source_of, receiver = mixed[0:count // 2 * 2:2], mixed[1:count // 2 * 2:2]
    room = jnp.minimum(lengths[source_of] - 1, limit - lengths[receiver]) // 2
    room = jnp.where((source_of == ranking[0]) | (receiver == ranking[0]) | (lengths[receiver] == 0), 0, jnp.maximum(room, 0))
    shifted = jax.random.randint(jax.random.fold_in(own, 4), (count // 2,), 0, 1 << 20) % (room + 1)
    lengths = lengths.at[source_of].add(-shifted).at[receiver].add(shifted)
    members = jnp.searchsorted(jnp.cumsum(lengths), jnp.arange(rows * top), side="right").astype(jnp.int32)
    table = members.reshape(top, rows).T
    table = table[jax.random.permutation(jax.random.fold_in(own, 1), rows)]
    turn = jax.random.randint(jax.random.fold_in(own, 2), (rows, 1), 0, top)
    return jnp.take_along_axis(table, (jnp.arange(top)[None, :] + turn) % top, axis=1)


def portions_of(number_of, total, bound, skew, full):
    portions = [(1 << 20) // math.isqrt(grade ** skew) + 1 for grade in range(1, number_of + 1)]
    largest = bound if full else min(bound, max(-(-total // number_of), total * portions[0] // sum(portions)))
    least = 1 if total - largest >= number_of - 1 else 0
    counts, rest = [largest] + [least] * (number_of - 1), total - largest - least * (number_of - 1)
    while rest > 0:
        free = [i for i in range(1, number_of) if counts[i] < largest] or [i for i in range(1, number_of) if counts[i] < bound]
        pool, left = sum([portions[i] for i in free]), rest
        for i in free:
            more = min(bound - counts[i], max(1, left * portions[i] // pool), rest)
            counts[i] = counts[i] + more
            rest = rest - more
    return np.array(counts)


def gaussian(key, dims, spread, limit, cuts=(), kind=jnp.bfloat16):
    loudness = steps_of(key, dims, cuts, -0.22, 0.18) if cuts else 1.0
    drawn = jax.random.normal(key, dims, jnp.float32) * spread * loudness
    return jnp.minimum(jnp.maximum(drawn, -limit), limit).astype(kind)


def setup_inputs(seed: int = 0) -> dict:
    key_of = jax.random.split(jax.random.key(seed), 12)
    queries = draw_queries(jax.random.fold_in(key_of[11], 71), 0)
    keys = draw_keys(jax.random.fold_in(key_of[11], 71), 0)
    values = gaussian(key_of[2], (SEQUENCE_TOKENS, KEY_VALUE_HEADS * HEAD_SIZE), 1.0, 6.0, ((0, 32),))
    out_proj = gaussian(key_of[3], (QUERY_HEADS * HEAD_SIZE, D), (QUERY_HEADS * HEAD_SIZE) ** -0.5, 0.09375, ((0, 16),))
    resid = draw_resid(jax.random.fold_in(key_of[11], 71), 0)
    norm_gain = jnp.clip(1.0 + 0.18 * jax.random.normal(key_of[5], (D,), jnp.float32), 0.1, 1.9)
    routes_keys = jax.random.split(jax.random.fold_in(key_of[6], 1), SEQUENCE_TOKENS // MOE_TOK)
    routes_turns = jax.random.permutation(jax.random.fold_in(key_of[6], 3), SEQUENCE_TOKENS // MOE_TOK)
    routes = jax.vmap(lambda own, number: routed_block(jax.random.fold_in(key_of[6], 2), own, number, MOE_TOK, EXPERTS, TOP, CAP, 2))(routes_keys, routes_turns).reshape((SEQUENCE_TOKENS, TOP))
    gates = jnp.clip(jnp.exp(math.log(1.0) - 2.9957323 * jax.random.uniform(key_of[7], (SEQUENCE_TOKENS, TOP), jnp.float32) ** steps_of(key_of[7], (SEQUENCE_TOKENS, TOP), ((0, 32),), -0.2, 0.2)), 0.05, 1.0)
    w_gate = gaussian(key_of[8], (EXPERTS, D, FF), D ** -0.5, 0.125, ((0, 16), (1, 32)))
    w_up = gaussian(key_of[9], (EXPERTS, D, FF), D ** -0.5, 0.125, ((0, 16), (1, 32)))
    w_down = gaussian(key_of[10], (EXPERTS, FF, D), FF ** -0.5, 0.21875, ((0, 16), (2, 32)))
    return {"queries": queries, "keys": keys, "values": values, "out_proj": out_proj, "resid": resid, "norm_gain": norm_gain, "routes": routes, "gates": gates, "w_gate": w_gate, "w_up": w_up, "w_down": w_down}


NEG = -1e+30

def attend_head(query_head, key_head, value_head):
    total = query_head.shape[0]
    block = math.gcd(total, 1024)
    scale = 1.0 / math.sqrt(query_head.shape[1])
    key_spots = jnp.arange(total, dtype=jnp.int32)

    def one_block(index):
        rows = lax.dynamic_slice_in_dim(query_head, index * block, block, 0)
        scores = jnp.dot(rows, key_head.T, preferred_element_type=jnp.float32) * scale
        spots = index * block + jnp.arange(block, dtype=jnp.int32)
        scores = jnp.where(key_spots[None, :] <= spots[:, None], scores, NEG)
        peak = lax.optimization_barrier(jnp.max(scores, axis=1, keepdims=True))
        weights = jnp.exp(scores - peak)
        mass = lax.optimization_barrier(jnp.sum(weights, axis=1, keepdims=True))
        summed = jnp.dot(weights.astype(jnp.bfloat16), value_head, preferred_element_type=jnp.float32)
        return summed / mass
    blocks = lax.map(one_block, jnp.arange(total // block, dtype=jnp.int32))
    return blocks.reshape(total, query_head.shape[1])

def reference(queries, keys, values, out_proj, resid, norm_gain, routes, gates, w_gate, w_up, w_down):
    query_group = QUERY_HEADS // KEY_VALUE_HEADS

    def head_step(head):
        shared = head // query_group
        query_head = lax.dynamic_slice_in_dim(queries, head * HEAD_SIZE, HEAD_SIZE, 1)
        key_head = lax.dynamic_slice_in_dim(keys, shared * HEAD_SIZE, HEAD_SIZE, 1)
        value_head = lax.dynamic_slice_in_dim(values, shared * HEAD_SIZE, HEAD_SIZE, 1)
        return attend_head(query_head, key_head, value_head)
    per_head = lax.map(head_step, jnp.arange(QUERY_HEADS, dtype=jnp.int32))
    attn = jnp.transpose(per_head, (1, 0, 2)).reshape(SEQUENCE_TOKENS, QUERY_HEADS * HEAD_SIZE).astype(jnp.bfloat16)
    width = QUERY_HEADS * HEAD_SIZE // N_EXP
    proj = jnp.zeros((SEQUENCE_TOKENS, D), jnp.float32)
    for group_index in range(N_EXP):
        lower = group_index * width
        part = jnp.dot(attn[:, lower:lower + width], out_proj[lower:lower + width], preferred_element_type=jnp.float32).astype(jnp.bfloat16)
        proj = proj + lax.optimization_barrier(part).astype(jnp.float32)
    hidden = resid.astype(jnp.float32) + proj
    normed = (hidden * lax.rsqrt(lax.optimization_barrier(jnp.mean(hidden * hidden, axis=1, keepdims=True)) + 1e-06) * norm_gain).astype(jnp.bfloat16)
    share = gates / lax.optimization_barrier(jnp.sum(gates, axis=1, keepdims=True))
    most = min(SEQUENCE_TOKENS, N_CTX * N_EXP * CAP)

    def expert_step(expert, mixture):
        chosen = routes == expert
        hit = jnp.any(chosen, axis=1)
        weight = lax.optimization_barrier(jnp.sum(jnp.where(chosen, share, 0.0), axis=1))
        slot = jnp.cumsum(hit.astype(jnp.int32), dtype=jnp.int32) - 1
        target = jnp.where(hit, slot, most)
        source = jnp.zeros((most,), jnp.int32).at[target].set(jnp.arange(SEQUENCE_TOKENS, dtype=jnp.int32), mode='drop')
        picked = normed[source]
        gate = jnp.dot(picked, w_gate[expert], preferred_element_type=jnp.float32)
        upward = jnp.dot(picked, w_up[expert], preferred_element_type=jnp.float32)
        act = (jax.nn.silu(gate) * upward).astype(jnp.bfloat16)
        expert_out = jnp.dot(act, w_down[expert], preferred_element_type=jnp.float32).astype(jnp.bfloat16)
        back = expert_out[jnp.clip(slot, 0, most - 1)].astype(jnp.float32)
        return mixture + jnp.where(hit[:, None], weight[:, None] * back, 0.0)
    mixture = lax.fori_loop(0, EXPERTS, expert_step, jnp.zeros((SEQUENCE_TOKENS, D), jnp.float32))
    layer_out = (hidden + mixture).astype(jnp.bfloat16)
    return (attn, layer_out)
```

```python
import math

import jax
import jax.numpy as jnp
from jax import lax
from jax.experimental import pallas as pl
from jax.experimental.pallas import tpu as pltpu
from jax.sharding import PartitionSpec as P

D = 2048
FF = 768
HEAD_SIZE = 128
KEY_HEAD_SHARERS = 4
SIDE = 4
RING = 16
TOKENS = 256
OWN = 16
HALF = D // 2
BLOCK = 1024
NEG = -1e30
F32 = jnp.float32
BF16 = jnp.bfloat16
MESH = pl.DeviceIdType.MESH


def wrap(index, size):
    return lax.rem(index + size, jnp.int32(size))


def remote(src, dst, sends, recvs, index, device):
    return pltpu.make_async_remote_copy(
        src_ref=src,
        dst_ref=dst,
        send_sem=sends.at[index],
        recv_sem=recvs.at[index],
        device_id=device,
        device_id_type=MESH,
    )


class TorusGather:
    def __init__(self, buf, sends, recvs, spot, devices, cut):
        first, second, core = spot
        to_first, to_second, to_core = devices
        up, down = wrap(first + 1, SIDE), wrap(first - 1, SIDE)
        above, below = wrap(second + 1, SIDE), wrap(second - 1, SIDE)
        across = wrap(second + 2, SIDE)
        size = buf.shape[3]
        own = buf.at[first, second, core]
        head = buf.at[down, second, core, pl.ds(0, cut)]
        tail = buf.at[up, second, core, pl.ds(cut, size - cut)]
        row = buf.at[:, second, core]
        row_head = buf.at[pl.ds(0, 2), below, core]
        row_tail = buf.at[pl.ds(2, 2), above, core]
        plan = [
            (own, to_first(up)),
            (own, to_first(down)),
            (head, to_first(up)),
            (tail, to_first(down)),
            (row, to_second(above)),
            (row, to_second(below)),
            (row_head, to_second(above)),
            (row_tail, to_second(below)),
            (row, to_core),
            (buf.at[:, below, core], to_core),
            (buf.at[:, above, core], to_core),
            (buf.at[:, across, core], to_core),
        ]
        self.copies = [
            remote(ref, ref, sends, recvs, index, device) for index, (ref, device) in enumerate(plan)
        ]

    def start(self, *which):
        for index in which:
            self.copies[index].start()

    def arrive(self, *which):
        for index in which:
            self.copies[index].wait_recv()

    def drain(self):
        for copy in self.copies:
            copy.wait_send()


class RingScatter:
    def __init__(self, terms, ring, sends, recvs, place):
        self.terms, self.ring, self.sends, self.recvs, self.place = terms, ring, sends, recvs, place
        self.next = ({"exp": wrap(place + 1, RING)}, {"exp": wrap(place - 1, RING)})

    def copy(self, way, step, half, src=None):
        src = self.ring.at[way, step, half] if src is None else src
        return remote(
            src,
            self.ring.at[way, step + 1, half],
            self.sends,
            self.recvs,
            (way, step, half),
            self.next[way],
        )

    def owner(self, way, step):
        return wrap(self.place + RING // 2 - step if way == 0 else self.place - RING // 2 + 1 + step, RING)

    def begin(self, half):
        for way in range(2):
            self.copy(way, 0, half, self.terms.at[self.owner(way, 0), half]).start()

    def advance(self, way, step, half):
        self.copy(way, step - 1, half).wait_recv()
        total = self.ring[way, step, half].astype(F32) + self.terms[self.owner(way, step), half].astype(F32)
        self.ring[way, step, half] = total.astype(BF16)
        self.copy(way, step, half).start()

    def run(self):
        def step(index, _):
            for half in range(2):
                for way in range(2):
                    self.advance(way, index, half)
            return 0

        lax.fori_loop(1, RING // 2 - 1, step, 0)
        for half in range(2):
            self.advance(0, RING // 2 - 1, half)

    def total(self, half):
        self.copy(0, RING // 2 - 1, half).wait_recv()
        self.copy(1, RING // 2 - 2, half).wait_recv()
        own = self.terms[self.place, half].astype(F32)
        return own + self.ring[0, RING // 2, half].astype(F32) + self.ring[1, RING // 2 - 1, half].astype(F32)

    def drain(self):
        def step(index, _):
            for half in range(2):
                for way in range(2):
                    self.copy(way, index, half).wait_send()
            return 0

        lax.fori_loop(0, RING // 2 - 1, step, 0)
        for half in range(2):
            self.copy(0, RING // 2 - 1, half).wait_send()


class RingGather:
    def __init__(self, rows, sends, recvs, place):
        self.rows, self.sends, self.recvs, self.place = rows, sends, recvs, place
        self.next = ({"exp": wrap(place + 1, RING)}, {"exp": wrap(place - 1, RING)})

    def copy(self, way, step, half):
        origin = wrap(self.place - step if way == 0 else self.place + step, RING)
        ref = self.rows.at[origin, half]
        return remote(ref, ref, self.sends, self.recvs, (way, step, half), self.next[way])

    def begin(self, half):
        for way in range(2):
            self.copy(way, 0, half).start()

    def run(self):
        def step(index, _):
            for half in range(2):
                for way in range(2):
                    self.copy(way, index - 1, half).wait_recv()
                    self.copy(way, index, half).start()
            return 0

        lax.fori_loop(1, RING // 2 - 1, step, 0)
        for half in range(2):
            self.copy(0, RING // 2 - 2, half).wait_recv()
            self.copy(0, RING // 2 - 1, half).start()
        for half in range(2):
            self.copy(1, RING // 2 - 2, half).wait_recv()
            self.copy(0, RING // 2 - 1, half).wait_recv()

    def drain(self):
        def step(index, _):
            for half in range(2):
                for way in range(2):
                    self.copy(way, index, half).wait_send()
            return 0

        lax.fori_loop(0, RING // 2 - 1, step, 0)
        for half in range(2):
            self.copy(0, RING // 2 - 1, half).wait_send()


def nt_dot(left, right):
    return lax.dot_general(left, right, (((1,), (1,)), ((), ())), preferred_element_type=F32)


def dot(left, right):
    return jnp.dot(left, right, preferred_element_type=F32)


def layer(
    queries, keys, values, out_proj, resid, gain, routes, gates, w_gate, w_up, w_down,
    attn_out, layer_out,
    kbuf, vbuf, abuf, bbuf, q_v, proj_v, resid_v, gain_v, routes_v, gates_v, weight_v, attn_v, hidden_v,
    terms, ring_one, normed, mixed, ring_two,
    loads, kv_sends, kv_recvs, w_sends, w_recvs, z_sends, z_recvs,
):
    ctx, place = lax.axis_index("ctx"), lax.axis_index("exp")
    x, y, core = lax.div(ctx, 8), lax.rem(lax.div(ctx, 2), 4), lax.rem(ctx, 2)

    def to_x(index):
        return {"ctx": index * 8 + y * 2 + core}

    def to_y(index):
        return {"ctx": x * 8 + index * 2 + core}

    to_core = {"ctx": x * 8 + y * 2 + (1 - core)}
    x_first = ((x, y, core), (to_x, to_y, to_core))
    y_first = ((y, x, core), (to_y, to_x, to_core))

    head_columns = pl.ds(pl.multiple_of(lax.div(place, KEY_HEAD_SHARERS) * HEAD_SIZE, HEAD_SIZE), HEAD_SIZE)
    own_rows = pl.ds(pl.multiple_of(place * OWN, OWN), OWN)
    own_a, own_b = abuf.at[x, y, core], bbuf.at[y, x, core]
    pairs = [
        (keys.at[:, head_columns], kbuf.at[x, y, core]),
        (values.at[:, head_columns], vbuf.at[y, x, core]),
        (queries, q_v),
        (w_gate, own_a.at[pl.ds(0, 64)]),
        (w_down.at[pl.ds(0, 32)], own_a.at[pl.ds(64, 32)]),
        (w_up, own_b.at[pl.ds(0, 64)]),
        (w_down.at[pl.ds(32, 32)], own_b.at[pl.ds(64, 32)]),
        (out_proj, proj_v),
        (resid.at[own_rows], resid_v),
        (gain, gain_v),
        (routes, routes_v),
        (gates, gates_v),
    ]
    local = [pltpu.make_async_copy(src, dst, loads.at[i]) for i, (src, dst) in enumerate(pairs)]
    for copy in local:
        copy.start()

    barrier = pltpu.get_barrier_semaphore()
    neighbours = [
        to_x(wrap(x + 1, SIDE)), to_x(wrap(x - 1, SIDE)), to_y(wrap(y + 1, SIDE)), to_y(wrap(y - 1, SIDE)),
        to_core, {"exp": wrap(place + 1, RING)}, {"exp": wrap(place - 1, RING)},
    ]
    for device in neighbours:
        pl.semaphore_signal(barrier, inc=1, device_id=device, device_id_type=MESH)
    pl.semaphore_wait(barrier, len(neighbours))

    k_gather = TorusGather(kbuf, kv_sends.at[0], kv_recvs.at[0], *x_first, 128)
    v_gather = TorusGather(vbuf, kv_sends.at[1], kv_recvs.at[1], *y_first, 128)
    a_gather = TorusGather(abuf, w_sends.at[0], w_recvs.at[0], *x_first, 48)
    b_gather = TorusGather(bbuf, w_sends.at[1], w_recvs.at[1], *y_first, 48)
    heads, experts = (k_gather, v_gather), (a_gather, b_gather)

    for index, gather in enumerate(heads):
        local[index].wait()
        gather.start(0, 1)
    for gather in heads:
        gather.arrive(0)
        gather.start(2)
        gather.arrive(1)
        gather.start(3)
    for gather in heads:
        gather.arrive(2, 3)
        gather.start(4, 5, 8)
    for copy in local[2:]:
        copy.wait()
    for gather in experts:
        gather.start(0, 1)
    for gather in heads:
        gather.arrive(4)
        gather.start(6, 9)
        gather.arrive(5)
        gather.start(7, 10)

    all_gates = gates_v[...]
    share = all_gates / jnp.sum(all_gates, axis=0, keepdims=True)
    here = jnp.sum(jnp.where(routes_v[...] == place, share, 0.0), axis=0, keepdims=True)
    weight_v[...] = jnp.broadcast_to(here, (128, TOKENS)).T

    for gather in heads:
        gather.arrive(6, 7)
        gather.start(11)
    for gather in experts:
        gather.arrive(0)
        gather.start(2)
        gather.arrive(1)
        gather.start(3)
    for gather in heads:
        gather.arrive(8, 9, 10, 11)

    query = jnp.concatenate([q_v[:, :HEAD_SIZE], q_v[:, HEAD_SIZE:]], axis=0)
    scale = math.log2(math.e) / math.sqrt(HEAD_SIZE)
    offset = lax.rem(ctx, 4) * TOKENS

    def visit(index, state, masked=False):
        peak, mass, accum = state
        far, near = lax.div(index, 2), lax.rem(index, 2) * 2
        some_keys = kbuf[far, pl.ds(near, 2)].reshape(BLOCK, HEAD_SIZE)
        some_values = vbuf[pl.ds(near, 2), far].reshape(BLOCK, HEAD_SIZE)
        scores = nt_dot(query, some_keys)
        if masked:
            row = lax.broadcasted_iota(jnp.int32, scores.shape, 0) & (TOKENS - 1)
            column = lax.broadcasted_iota(jnp.int32, scores.shape, 1)
            scores = jnp.where(column <= row + offset, scores, NEG)
        new_peak = jnp.maximum(peak, jnp.max(scores, axis=1, keepdims=True))
        weights = jnp.exp2((scores - new_peak) * scale)
        fade = jnp.exp2((peak - new_peak) * scale)
        part = weights[:, :128]
        for low in range(128, BLOCK, 128):
            part = part + weights[:, low : low + 128]
        mass = mass * fade + part
        accum = accum * fade + dot(weights.astype(BF16), some_values)
        return (new_peak, mass, accum)

    last = lax.div(ctx, 4)
    middle = lax.div(last, 2)
    state = (
        jnp.full((2 * TOKENS, 1), NEG, F32),
        jnp.zeros((2 * TOKENS, 128), F32),
        jnp.zeros((2 * TOKENS, HEAD_SIZE), F32),
    )
    state = lax.fori_loop(0, middle, visit, state)
    for gather in experts:
        gather.arrive(2, 3)
        gather.start(4, 5, 8)
    state = lax.fori_loop(middle, last, visit, state)
    _, mass, accum = visit(last, state, masked=True)
    result = (accum / jnp.sum(mass, axis=1, keepdims=True)).astype(BF16)
    attn_v[:, :HEAD_SIZE] = result[:TOKENS]
    attn_v[:, HEAD_SIZE:] = result[TOKENS:]
    attn_copy = pltpu.make_async_copy(attn_v, attn_out, loads.at[len(pairs)])
    attn_copy.start()

    scatter_one = RingScatter(terms, ring_one, z_sends.at[0], z_recvs.at[0], place)
    for half in range(2):
        term = dot(attn_v[...], proj_v[:, half * HALF : (half + 1) * HALF])
        terms[:, half] = term.astype(BF16).reshape(RING, OWN, HALF)
        scatter_one.begin(half)
    for gather in experts:
        gather.arrive(4)
        gather.start(6, 9)
        gather.arrive(5)
        gather.start(7, 10)
    scatter_one.run()
    for half in range(2):
        columns = slice(half * HALF, (half + 1) * HALF)
        hidden_v[:, columns] = resid_v[:, columns].astype(F32) + scatter_one.total(half)

    hidden = hidden_v[...]
    spread = lax.rsqrt(jnp.mean(hidden * hidden, axis=1, keepdims=True) + 1e-06)
    rows = (hidden * spread * gain_v[...]).astype(BF16)
    spread_rows = RingGather(normed, z_sends.at[1], z_recvs.at[1], place)
    for half in range(2):
        normed[place, half] = rows[:, half * HALF : (half + 1) * HALF]
        spread_rows.begin(half)
    for gather in experts:
        gather.arrive(6, 7)
        gather.start(11)
    spread_rows.run()
    for gather in experts:
        gather.arrive(8, 9, 10, 11)

    gate_sum = jnp.zeros((TOKENS, FF), F32)
    for half in range(2):
        part = normed[:, half].reshape(TOKENS, HALF)
        gate_sum += dot(part, abuf[2 * half : 2 * half + 2, :, :, :64].reshape(HALF, FF))
    up_sum = jnp.zeros((TOKENS, FF), F32)
    for quarter in range(SIDE):
        low = quarter % 2 * 512
        part = normed[:, quarter // 2, :, low : low + 512].reshape(TOKENS, 512)
        up_sum += dot(part, bbuf[:, quarter, :, :64].reshape(512, FF))
    act = (gate_sum / (1.0 + jnp.exp(-gate_sum)) * up_sum).astype(BF16)
    weight = weight_v[:, :1]
    scatter_two = RingScatter(mixed, ring_two, z_sends.at[2], z_recvs.at[2], place)
    for quarter in range(SIDE):
        low = quarter % 2 * 512
        down = jnp.concatenate([abuf[quarter, :, :, 64:], bbuf[:, quarter, :, 64:]], axis=2)
        part = nt_dot(act, down.reshape(512, FF)).astype(BF16).astype(F32)
        part = jnp.where(weight > 0.0, weight * part, 0.0).astype(BF16)
        mixed[:, quarter // 2, :, low : low + 512] = part.reshape(RING, OWN, 512)
        if quarter % 2:
            scatter_two.begin(quarter // 2)
    scatter_two.run()
    for half in range(2):
        columns = slice(half * HALF, (half + 1) * HALF)
        layer_out[:, columns] = (hidden_v[:, columns] + scatter_two.total(half)).astype(BF16)

    attn_copy.wait()
    for gather in (*heads, *experts, scatter_one, spread_rows, scatter_two):
        gather.drain()


def local_layer(queries, keys, values, out_proj, resid, norm_gain, routes, gates, w_gate, w_up, w_down):
    anywhere = pl.BlockSpec(memory_space=pl.ANY)
    torus = (SIDE, SIDE, 2)
    pieces = (RING, 2, OWN, HALF)
    ring = (2, RING // 2 + 1, 2, OWN, HALF)
    ring_sems = pltpu.SemaphoreType.DMA((3, 2, RING // 2, 2))
    gather_sems = pltpu.SemaphoreType.DMA((2, 12))
    return pl.pallas_call(
        layer,
        out_shape=(
            jax.ShapeDtypeStruct(queries.shape, BF16),
            jax.ShapeDtypeStruct((OWN, D), BF16),
        ),
        in_specs=[anywhere] * 11,
        out_specs=(anywhere, pl.BlockSpec(memory_space=pltpu.VMEM)),
        scratch_shapes=[
            pltpu.VMEM((*torus, TOKENS, HEAD_SIZE), BF16),
            pltpu.VMEM((*torus, TOKENS, HEAD_SIZE), BF16),
            pltpu.VMEM((*torus, 96, FF), BF16),
            pltpu.VMEM((*torus, 96, FF), BF16),
            pltpu.VMEM(queries.shape, BF16),
            pltpu.VMEM(out_proj.shape, BF16),
            pltpu.VMEM((OWN, D), BF16),
            pltpu.VMEM((1, D), F32),
            pltpu.VMEM((8, TOKENS), jnp.int32),
            pltpu.VMEM((8, TOKENS), F32),
            pltpu.VMEM((TOKENS, 128), F32),
            pltpu.VMEM(queries.shape, BF16),
            pltpu.VMEM((OWN, D), F32),
            pltpu.VMEM(pieces, BF16),
            pltpu.VMEM(ring, BF16),
            pltpu.VMEM(pieces, BF16),
            pltpu.VMEM(pieces, BF16),
            pltpu.VMEM(ring, BF16),
            pltpu.SemaphoreType.DMA((13,)),
            gather_sems,
            gather_sems,
            gather_sems,
            gather_sems,
            ring_sems,
            ring_sems,
        ],
        compiler_params=pltpu.CompilerParams(
            collective_id=0, has_side_effects=True, vmem_limit_bytes=56 * 1024 * 1024
        ),
        name="layer",
    )(
        queries,
        keys,
        values,
        out_proj,
        resid,
        norm_gain.reshape(1, D),
        routes.T,
        gates.T,
        w_gate[0],
        w_up[0],
        w_down[0].T,
    )


def solution(mesh):
    placed = (
        P("ctx", "exp"),
        P("ctx", None),
        P("ctx", None),
        P("exp", None),
        P("ctx", None),
        P(),
        P("ctx", None),
        P("ctx", None),
        P("exp", "ctx", None),
        P("exp", "ctx", None),
        P("exp", None, "ctx"),
    )
    return jax.shard_map(
        local_layer,
        mesh=mesh,
        in_specs=placed,
        out_specs=(P("ctx", "exp"), P(("ctx", "exp"), None)),
        check_vma=False,
    )
```

```python
import math

import jax
import jax.numpy as jnp
from jax import lax
from jax.experimental import pallas as pl
from jax.experimental.pallas import tpu as pltpu
from jax.sharding import PartitionSpec as P

D = 2048
FF = 768
HEAD_SIZE = 128
KEY_HEAD_SHARERS = 4
SIDE = 4
RING = 16
TOKENS = 256
OWN = 16
HALF = D // 2
PART = OWN // 2
BLOCK = 2048
NEG = -1e30
F32 = jnp.float32
BF16 = jnp.bfloat16
MESH = pl.DeviceIdType.MESH


def wrap(index, size):
    return lax.rem(index + size, jnp.int32(size))


def remote(src, dst, sends, recvs, index, device):
    return pltpu.make_async_remote_copy(
        src_ref=src,
        dst_ref=dst,
        send_sem=sends.at[index],
        recv_sem=recvs.at[index],
        device_id=device,
        device_id_type=MESH,
    )


class TorusGather:
    def __init__(self, buf, sends, recvs, spot, devices, cut):
        first, second, core = spot
        to_first, to_second, to_core = devices
        up, down = wrap(first + 1, SIDE), wrap(first - 1, SIDE)
        above, below = wrap(second + 1, SIDE), wrap(second - 1, SIDE)
        across = wrap(second + 2, SIDE)
        size = buf.shape[3]
        own = buf.at[first, second, core]
        head = buf.at[down, second, core, pl.ds(0, cut)]
        tail = buf.at[up, second, core, pl.ds(cut, size - cut)]
        row = buf.at[:, second, core]
        row_head = buf.at[pl.ds(0, 2), below, core]
        row_tail = buf.at[pl.ds(2, 2), above, core]
        plan = [
            (own, to_first(up)),
            (own, to_first(down)),
            (head, to_first(up)),
            (tail, to_first(down)),
            (row, to_second(above)),
            (row, to_second(below)),
            (row_head, to_second(above)),
            (row_tail, to_second(below)),
            (row, to_core),
            (buf.at[:, below, core], to_core),
            (buf.at[:, above, core], to_core),
            (buf.at[:, across, core], to_core),
        ]
        self.copies = [
            remote(ref, ref, sends, recvs, index, device) for index, (ref, device) in enumerate(plan)
        ]

    def start(self, *which):
        for index in which:
            self.copies[index].start()

    def arrive(self, *which):
        for index in which:
            self.copies[index].wait_recv()

    def drain(self):
        for copy in self.copies:
            copy.wait_send()


class RingScatter:
    def __init__(self, terms, ring, sends, recvs, place):
        self.terms, self.ring, self.sends, self.recvs, self.place = terms, ring, sends, recvs, place

    def copy(self, way, far, step, src=None):
        dst = self.ring.at[way, far, step]
        sign = 1 - 2 * way
        device = {"exp": wrap(self.place + sign * (1 + far), RING)}
        return remote(dst if src is None else src, dst, self.sends, self.recvs, (way, far, step), device)

    def term(self, way, distance):
        return self.terms.at[wrap(self.place + (1 - 2 * way) * distance, RING)]

    def begin(self):
        self.copy(0, 1, 3, self.term(0, 8)).start()
        for step in (3, 2, 1, 0):
            for way in range(2):
                self.copy(way, 0, step, self.term(way, 2 * step + 1)).start()

    def arrived(self, way, step):
        self.copy(way, 0, step).wait_recv()
        total = self.ring[way, 0, step].astype(F32)
        if way == 0 or step < 3:
            self.copy(way, 1, step).wait_recv()
            total += self.ring[way, 1, step].astype(F32)
        return total

    def relay(self, step):
        for way in range(2):
            total = self.arrived(way, step) + self.term(way, 2 * step)[...].astype(F32)
            self.ring[way, 1, step] = total.astype(BF16)
            self.copy(way, 1, step - 1, self.ring.at[way, 1, step]).start()

    def total(self):
        return self.terms[self.place].astype(F32) + self.arrived(0, 0) + self.arrived(1, 0)

    def drain(self):
        for way in range(2):
            for step in range(4):
                self.copy(way, 0, step).wait_send()
                if way == 0 or step < 3:
                    self.copy(way, 1, step).wait_send()


class RingGather:
    def __init__(self, rows, sends, recvs, place):
        self.rows, self.sends, self.recvs, self.place = rows, sends, recvs, place

    def copy(self, way, far, step):
        sign = 1 - 2 * way
        ref = self.rows.at[wrap(self.place - sign * 2 * step, RING)]
        device = {"exp": wrap(self.place + sign * (1 + far), RING)}
        return remote(ref, ref, self.sends, self.recvs, (way, far, step), device)

    def send(self, step):
        for way in range(2):
            if way == 0 or step < 3:
                self.copy(way, 1, step).start()
        for way in range(2):
            self.copy(way, 0, step).start()

    def relay(self, step):
        for way in range(2):
            self.copy(way, 1, step - 1).wait_recv()
        self.send(step)

    def finish(self):
        for way in range(2):
            for step in range(4):
                self.copy(way, 0, step).wait_recv()
        self.copy(0, 1, 3).wait_recv()

    def drain(self):
        for way in range(2):
            for step in range(4):
                self.copy(way, 0, step).wait_send()
                if way == 0 or step < 3:
                    self.copy(way, 1, step).wait_send()


def pack(left, right):
    parts = [half.reshape(RING, PART, half.shape[1]) for half in (left, right)]
    return jnp.concatenate(parts, axis=1).astype(BF16)


def unpack(pieces):
    wide = pieces.astype(F32)
    width = wide.shape[2]
    return [wide[:, low : low + PART].reshape(RING * PART, width).astype(BF16) for low in (0, PART)]


def part_rows(rows, part):
    wide = rows.astype(F32).reshape(RING, OWN, rows.shape[1])
    return wide[:, part * PART : (part + 1) * PART].reshape(RING * PART, rows.shape[1])


def nt_dot(left, right):
    return lax.dot_general(left, right, (((1,), (1,)), ((), ())), preferred_element_type=F32)


def dot(left, right):
    return jnp.dot(left, right, preferred_element_type=F32)


def layer(
    queries, keys, values, out_proj, resid, gain, routes, gates, w_gate, w_up, w_down,
    attn_out, layer_out,
    kbuf, vbuf, abuf, bbuf, q_v, proj_v, resid_v, gain_v, routes_v, gates_v, weight_v, attn_v,
    terms, ring_one, normed, mixed, ring_two,
    loads, kv_sends, kv_recvs, w_sends, w_recvs, z_sends, z_recvs,
):
    ctx, place = lax.axis_index("ctx"), lax.axis_index("exp")
    x, y, core = lax.div(ctx, 8), lax.rem(lax.div(ctx, 2), 4), lax.rem(ctx, 2)

    def to_x(index):
        return {"ctx": index * 8 + y * 2 + core}

    def to_y(index):
        return {"ctx": x * 8 + index * 2 + core}

    to_core = {"ctx": x * 8 + y * 2 + (1 - core)}
    x_first = ((x, y, core), (to_x, to_y, to_core))
    y_first = ((y, x, core), (to_y, to_x, to_core))

    head_columns = pl.ds(pl.multiple_of(lax.div(place, KEY_HEAD_SHARERS) * HEAD_SIZE, HEAD_SIZE), HEAD_SIZE)
    own_rows = pl.ds(pl.multiple_of(place * OWN, OWN), OWN)
    own_a, own_b = abuf.at[x, y, core], bbuf.at[y, x, core]
    pairs = [
        (keys.at[:, head_columns], kbuf.at[x, y, core]),
        (values.at[:, head_columns], vbuf.at[y, x, core]),
        (queries, q_v),
        (w_gate, own_a.at[pl.ds(0, 64)]),
        (w_down.at[pl.ds(0, 32)], own_a.at[pl.ds(64, 32)]),
        (w_up, own_b.at[pl.ds(0, 64)]),
        (w_down.at[pl.ds(32, 32)], own_b.at[pl.ds(64, 32)]),
        (out_proj, proj_v),
        (resid.at[own_rows], resid_v),
        (gain, gain_v),
        (routes, routes_v),
        (gates, gates_v),
    ]
    local = [pltpu.make_async_copy(src, dst, loads.at[i]) for i, (src, dst) in enumerate(pairs)]
    for copy in local:
        copy.start()

    barrier = pltpu.get_barrier_semaphore()
    neighbours = [to_x(wrap(x + 1, SIDE)), to_x(wrap(x - 1, SIDE)), to_y(wrap(y + 1, SIDE)), to_y(wrap(y - 1, SIDE))]
    neighbours += [to_core] + [{"exp": wrap(place + far, RING)} for far in (1, -1, 2, -2)]
    for device in neighbours:
        pl.semaphore_signal(barrier, inc=1, device_id=device, device_id_type=MESH)
    pl.semaphore_wait(barrier, len(neighbours))

    k_gather = TorusGather(kbuf, kv_sends.at[0], kv_recvs.at[0], *x_first, 128)
    v_gather = TorusGather(vbuf, kv_sends.at[1], kv_recvs.at[1], *y_first, 128)
    a_gather = TorusGather(abuf, w_sends.at[0], w_recvs.at[0], *x_first, 48)
    b_gather = TorusGather(bbuf, w_sends.at[1], w_recvs.at[1], *y_first, 48)
    heads, experts = (k_gather, v_gather), (a_gather, b_gather)

    for index, gather in enumerate(heads):
        local[index].wait()
        gather.start(0, 1)
    for gather in heads:
        gather.arrive(0)
        gather.start(2)
        gather.arrive(1)
        gather.start(3)
    for gather in heads:
        gather.arrive(2, 3)
        gather.start(4, 5, 8)
    for copy in local[2:]:
        copy.wait()
    for gather in experts:
        gather.start(0, 1)
    for gather in heads:
        gather.arrive(4)
        gather.start(6, 9)
        gather.arrive(5)
        gather.start(7, 10)

    all_gates = gates_v[...]
    share = all_gates / jnp.sum(all_gates, axis=0, keepdims=True)
    here = jnp.sum(jnp.where(routes_v[...] == place, share, 0.0), axis=0, keepdims=True)
    weight_v[...] = jnp.broadcast_to(here, (128, TOKENS)).T

    for gather in heads:
        gather.arrive(6, 7)
        gather.start(11)
    for gather in experts:
        gather.arrive(0)
        gather.start(2)
        gather.arrive(1)
        gather.start(3)
    for gather in heads:
        gather.arrive(8, 9, 10, 11)

    scale = math.log2(math.e) / math.sqrt(HEAD_SIZE)
    offset = lax.rem(ctx, 8) * TOKENS
    half_rows = RING * PART

    def query_of(part):
        rows = part_rows(q_v[...], part)
        return jnp.concatenate([rows[:, :HEAD_SIZE], rows[:, HEAD_SIZE:]], axis=0).astype(BF16)

    def visit(query, part, index, state, masked=False):
        peak, mass, accum = state
        some_keys = kbuf[index].reshape(BLOCK, HEAD_SIZE)
        some_values = vbuf[:, index].reshape(BLOCK, HEAD_SIZE)
        scores = nt_dot(query, some_keys)
        if masked:
            row = lax.broadcasted_iota(jnp.int32, (2 * half_rows, 1), 0) & (half_rows - 1)
            token = (row >> 3) * OWN + (row & (PART - 1)) + part * PART + offset
            column = lax.broadcasted_iota(jnp.int32, scores.shape, 1)
            scores = jnp.where(column <= token, scores, NEG)
        new_peak = jnp.maximum(peak, jnp.max(scores, axis=1, keepdims=True))
        weights = jnp.exp2((scores - new_peak) * scale)
        fade = jnp.exp2((peak - new_peak) * scale)
        some = weights[:, :128]
        for low in range(128, BLOCK, 128):
            some = some + weights[:, low : low + 128]
        mass = mass * fade + some
        accum = accum * fade + dot(weights.astype(BF16), some_values)
        return (new_peak, mass, accum)

    middle = lax.div(x + 1, 2)

    def first_blocks(part):
        state = (
            jnp.full((2 * half_rows, 1), NEG, F32),
            jnp.zeros((2 * half_rows, 128), F32),
            jnp.zeros((2 * half_rows, HEAD_SIZE), F32),
        )
        return lax.fori_loop(0, middle, lambda index, state: visit(query_of(part), part, index, state), state)

    def last_blocks(part, state):
        state = lax.fori_loop(middle, x, lambda index, state: visit(query_of(part), part, index, state), state)
        _, mass, accum = visit(query_of(part), part, x, state, masked=True)
        result = accum / jnp.sum(mass, axis=1, keepdims=True)
        return jnp.concatenate([result[:half_rows], result[half_rows:]], axis=1)

    def project(part, rows):
        halves = [dot(rows.astype(BF16), proj_v[:, low : low + HALF]) for low in (0, HALF)]
        terms[part] = pack(*halves)

    def norm(part):
        total = scatter_one[part].total()
        rows = resid_v[...].astype(F32)[part * PART : (part + 1) * PART]
        hidden = rows + jnp.concatenate([total[:PART], total[PART:]], axis=1)
        spread = lax.rsqrt(jnp.mean(hidden * hidden, axis=1, keepdims=True) + 1e-06)
        own = hidden * spread * gain_v[...]
        normed[part, place] = jnp.concatenate([own[:, :HALF], own[:, HALF:]], axis=0).astype(BF16)
        return hidden

    def expert(part):
        left, right = unpack(normed[part])
        gate_sum = dot(left, abuf[:2, :, :, :64].reshape(HALF, FF))
        gate_sum += dot(right, abuf[2:, :, :, :64].reshape(HALF, FF))
        up_sum = jnp.zeros(gate_sum.shape, F32)
        for quarter in range(SIDE):
            low = quarter % 2 * 512
            some = (left, right)[quarter // 2][:, low : low + 512]
            up_sum += dot(some, bbuf[:, quarter, :, :64].reshape(512, FF))
        act = (gate_sum / (1.0 + jnp.exp(-gate_sum)) * up_sum).astype(BF16)
        weight = part_rows(weight_v[...], part)[:, :1]

        def down(quarter):
            rows = jnp.concatenate([abuf[quarter, :, :, 64:], bbuf[:, quarter, :, 64:]], axis=2)
            some = nt_dot(act, rows.reshape(512, FF)).astype(BF16).astype(F32)
            return jnp.where(weight > 0.0, weight * some, 0.0)

        for low in range(2):
            mixed[part, :, :, low * 512 : low * 512 + 512] = pack(down(low), down(low + 2))

    scatter_one = [RingScatter(terms.at[i], ring_one.at[i], z_sends.at[i], z_recvs.at[i], place) for i in range(2)]
    spread_rows = [RingGather(normed.at[i], z_sends.at[2 + i], z_recvs.at[2 + i], place) for i in range(2)]
    scatter_two = [
        RingScatter(mixed.at[i], ring_two.at[i], z_sends.at[4 + i], z_recvs.at[4 + i], place) for i in range(2)
    ]

    state = first_blocks(0)
    for gather in experts:
        gather.arrive(2, 3)
        gather.start(4, 5, 8)
    early = last_blocks(0, state)
    project(0, early)
    scatter_one[0].begin()
    state = first_blocks(1)
    scatter_one[0].relay(3)
    late = last_blocks(1, state)
    scatter_one[0].relay(2)
    project(1, late)
    scatter_one[1].begin()
    pair = [rows.reshape(RING, PART, 2 * HEAD_SIZE) for rows in (early, late)]
    attn_v[...] = jnp.concatenate(pair, axis=1).reshape(TOKENS, 2 * HEAD_SIZE).astype(BF16)
    attn_copy = pltpu.make_async_copy(attn_v, attn_out, loads.at[len(pairs)])
    attn_copy.start()
    scatter_one[0].relay(1)
    for gather in experts:
        gather.arrive(4)
        gather.start(6, 9)
        gather.arrive(5)
        gather.start(7, 10)
    scatter_one[1].relay(3)
    hidden_early = norm(0)
    spread_rows[0].send(0)
    scatter_one[1].relay(2)
    spread_rows[0].relay(1)
    scatter_one[1].relay(1)
    for gather in experts:
        gather.arrive(6, 7)
        gather.start(11)
    spread_rows[0].relay(2)
    hidden_late = norm(1)
    spread_rows[1].send(0)
    spread_rows[0].relay(3)
    spread_rows[1].relay(1)
    for gather in experts:
        gather.arrive(8, 9, 10, 11)
    spread_rows[0].finish()
    expert(0)
    scatter_two[0].begin()
    spread_rows[1].relay(2)
    scatter_two[0].relay(3)
    spread_rows[1].relay(3)
    scatter_two[0].relay(2)
    spread_rows[1].finish()
    expert(1)
    scatter_two[1].begin()
    scatter_two[0].relay(1)
    scatter_two[1].relay(3)
    done = []
    for part, hidden in enumerate((hidden_early, hidden_late)):
        total = scatter_two[part].total()
        done.append(hidden + jnp.concatenate([total[:PART], total[PART:]], axis=1))
        if part == 0:
            scatter_two[1].relay(2)
            scatter_two[1].relay(1)
    layer_out[...] = jnp.concatenate(done, axis=0).astype(BF16)

    attn_copy.wait()
    for gather in (*heads, *experts, *scatter_one, *spread_rows, *scatter_two):
        gather.drain()


def local_layer(queries, keys, values, out_proj, resid, norm_gain, routes, gates, w_gate, w_up, w_down):
    anywhere = pl.BlockSpec(memory_space=pl.ANY)
    torus = (SIDE, SIDE, 2)
    pieces = (2, RING, 2 * PART, HALF)
    ring = (2, 2, 2, 4, 2 * PART, HALF)
    ring_sems = pltpu.SemaphoreType.DMA((6, 2, 2, 4))
    gather_sems = pltpu.SemaphoreType.DMA((2, 12))
    return pl.pallas_call(
        layer,
        out_shape=(
            jax.ShapeDtypeStruct(queries.shape, BF16),
            jax.ShapeDtypeStruct((OWN, D), BF16),
        ),
        in_specs=[anywhere] * 11,
        out_specs=(anywhere, pl.BlockSpec(memory_space=pltpu.VMEM)),
        scratch_shapes=[
            pltpu.VMEM((*torus, TOKENS, HEAD_SIZE), BF16),
            pltpu.VMEM((*torus, TOKENS, HEAD_SIZE), BF16),
            pltpu.VMEM((*torus, 96, FF), BF16),
            pltpu.VMEM((*torus, 96, FF), BF16),
            pltpu.VMEM(queries.shape, BF16),
            pltpu.VMEM(out_proj.shape, BF16),
            pltpu.VMEM((OWN, D), BF16),
            pltpu.VMEM((1, D), F32),
            pltpu.VMEM((8, TOKENS), jnp.int32),
            pltpu.VMEM((8, TOKENS), F32),
            pltpu.VMEM((TOKENS, 128), F32),
            pltpu.VMEM(queries.shape, BF16),
            pltpu.VMEM(pieces, BF16),
            pltpu.VMEM(ring, BF16),
            pltpu.VMEM(pieces, BF16),
            pltpu.VMEM(pieces, BF16),
            pltpu.VMEM(ring, BF16),
            pltpu.SemaphoreType.DMA((13,)),
            gather_sems,
            gather_sems,
            gather_sems,
            gather_sems,
            ring_sems,
            ring_sems,
        ],
        compiler_params=pltpu.CompilerParams(
            collective_id=0, has_side_effects=True, vmem_limit_bytes=56 * 1024 * 1024
        ),
        name="layer",
    )(
        queries,
        keys,
        values,
        out_proj,
        resid,
        norm_gain.reshape(1, D),
        routes.T,
        gates.T,
        w_gate[0],
        w_up[0],
        w_down[0].T,
    )


def solution(mesh):
    placed = (
        P("ctx", "exp"),
        P("ctx", None),
        P("ctx", None),
        P("exp", None),
        P("ctx", None),
        P(),
        P("ctx", None),
        P("ctx", None),
        P("exp", "ctx", None),
        P("exp", "ctx", None),
        P("exp", None, "ctx"),
    )
    return jax.shard_map(
        local_layer,
        mesh=mesh,
        in_specs=placed,
        out_specs=(P("ctx", "exp"), P(("ctx", "exp"), None)),
        check_vma=False,
    )
```

```python
import math

import jax
import jax.numpy as jnp
from jax import lax
from jax.experimental import pallas as pl
from jax.experimental.pallas import tpu as pltpu
from jax.sharding import PartitionSpec as P

D = 2048
FF = 768
HEAD_SIZE = 128
KEY_HEAD_SHARERS = 4
SIDE = 4
RING = 16
TOKENS = 256
OWN = 16
HALF = D // 2
PART = OWN // 2
BLOCK = 2048
NEG = -1e30
F32 = jnp.float32
BF16 = jnp.bfloat16
MESH = pl.DeviceIdType.MESH


def wrap(index, size):
    return lax.rem(index + size, jnp.int32(size))


def remote(src, dst, sends, recvs, index, device):
    return pltpu.make_async_remote_copy(
        src_ref=src,
        dst_ref=dst,
        send_sem=sends.at[index],
        recv_sem=recvs.at[index],
        device_id=device,
        device_id_type=MESH,
    )


class TorusGather:
    def __init__(self, buf, sends, recvs, spot, devices):
        first, second, core = spot
        to_first, to_second, to_core = devices
        above, below = wrap(second + 1, SIDE), wrap(second - 1, SIDE)
        self.rows = (second, below, above, wrap(second + 2, SIDE))
        own = buf.at[first, second, core]
        row = buf.at[:, second, core]
        plan = [(own, to_first(wrap(first + far, SIDE))) for far in (1, -1, 2)]
        plan += [
            (row, to_second(above)),
            (row, to_second(below)),
            (buf.at[pl.ds(0, 2), below, core], to_second(above)),
            (buf.at[pl.ds(2, 2), above, core], to_second(below)),
        ]
        plan += [(buf.at[:, other, core], to_core) for other in self.rows]
        self.copies = [
            remote(ref, ref, sends, recvs, index, device) for index, (ref, device) in enumerate(plan)
        ]

    def start(self, *which):
        for index in which:
            self.copies[index].start()

    def arrive(self, *which):
        for index in which:
            self.copies[index].wait_recv()

    def drain(self):
        for copy in self.copies:
            copy.wait_send()


class RingScatter:
    def __init__(self, terms, ring, sends, recvs, place):
        self.terms, self.ring, self.sends, self.recvs, self.place = terms, ring, sends, recvs, place

    def copy(self, way, far, step, src=None):
        dst = self.ring.at[way, far, step]
        sign = 1 - 2 * way
        device = {"exp": wrap(self.place + sign * (1 + far), RING)}
        return remote(dst if src is None else src, dst, self.sends, self.recvs, (way, far, step), device)

    def term(self, way, distance):
        return self.terms.at[wrap(self.place + (1 - 2 * way) * distance, RING)]

    def begin(self):
        self.copy(0, 1, 3, self.term(0, 8)).start()
        for step in (3, 2, 1, 0):
            for way in range(2):
                self.copy(way, 0, step, self.term(way, 2 * step + 1)).start()

    def arrived(self, way, step):
        self.copy(way, 0, step).wait_recv()
        total = self.ring[way, 0, step].astype(F32)
        if way == 0 or step < 3:
            self.copy(way, 1, step).wait_recv()
            total += self.ring[way, 1, step].astype(F32)
        return total

    def relay(self, step):
        for way in range(2):
            total = self.arrived(way, step) + self.term(way, 2 * step)[...].astype(F32)
            self.ring[way, 1, step] = total.astype(BF16)
            self.copy(way, 1, step - 1, self.ring.at[way, 1, step]).start()

    def total(self):
        return self.terms[self.place].astype(F32) + self.arrived(0, 0) + self.arrived(1, 0)

    def drain(self):
        for way in range(2):
            for step in range(4):
                self.copy(way, 0, step).wait_send()
                if way == 0 or step < 3:
                    self.copy(way, 1, step).wait_send()


class RingGather:
    def __init__(self, rows, sends, recvs, place):
        self.rows, self.sends, self.recvs, self.place = rows, sends, recvs, place

    def copy(self, way, far, step):
        sign = 1 - 2 * way
        ref = self.rows.at[wrap(self.place - sign * 2 * step, RING)]
        device = {"exp": wrap(self.place + sign * (1 + far), RING)}
        return remote(ref, ref, self.sends, self.recvs, (way, far, step), device)

    def send(self, step):
        for way in range(2):
            if way == 0 or step < 3:
                self.copy(way, 1, step).start()
        for way in range(2):
            self.copy(way, 0, step).start()

    def relay(self, step):
        for way in range(2):
            self.copy(way, 1, step - 1).wait_recv()
        self.send(step)

    def finish(self):
        for way in range(2):
            for step in range(4):
                self.copy(way, 0, step).wait_recv()
        self.copy(0, 1, 3).wait_recv()

    def drain(self):
        for way in range(2):
            for step in range(4):
                self.copy(way, 0, step).wait_send()
                if way == 0 or step < 3:
                    self.copy(way, 1, step).wait_send()


def pack(left, right):
    parts = [half.reshape(RING, PART, half.shape[1]) for half in (left, right)]
    return jnp.concatenate(parts, axis=1).astype(BF16)


def unpack(pieces):
    wide = pieces.astype(F32)
    width = wide.shape[2]
    return [wide[:, low : low + PART].reshape(RING * PART, width).astype(BF16) for low in (0, PART)]


def part_rows(rows, part):
    wide = rows.astype(F32).reshape(RING, OWN, rows.shape[1])
    return wide[:, part * PART : (part + 1) * PART].reshape(RING * PART, rows.shape[1])


def nt_dot(left, right):
    return lax.dot_general(left, right, (((1,), (1,)), ((), ())), preferred_element_type=F32)


def dot(left, right):
    return jnp.dot(left, right, preferred_element_type=F32)


def layer(
    queries, keys, values, out_proj, resid, gain, routes, gates, w_gate, w_up, w_down,
    attn_out, layer_out,
    heads_x, heads_y, abuf, bbuf, q_v, proj_v, resid_v, gain_v, routes_v, gates_v, weight_v, attn_v,
    terms, ring_one, normed, mixed, ring_two,
    loads, kv_sends, kv_recvs, w_sends, w_recvs, z_sends, z_recvs,
):
    ctx, place = lax.axis_index("ctx"), lax.axis_index("exp")
    x, y, core = lax.div(ctx, 8), lax.rem(lax.div(ctx, 2), 4), lax.rem(ctx, 2)

    def to_x(index):
        return {"ctx": index * 8 + y * 2 + core}

    def to_y(index):
        return {"ctx": x * 8 + index * 2 + core}

    to_core = {"ctx": x * 8 + y * 2 + (1 - core)}
    x_first = ((x, y, core), (to_x, to_y, to_core))
    y_first = ((y, x, core), (to_y, to_x, to_core))

    head_columns = pl.ds(pl.multiple_of(lax.div(place, KEY_HEAD_SHARERS) * HEAD_SIZE, HEAD_SIZE), HEAD_SIZE)
    own_rows = pl.ds(pl.multiple_of(place * OWN, OWN), OWN)
    own_a, own_b = abuf.at[x, y, core], bbuf.at[y, x, core]
    half_rows = RING * PART
    pairs = [
        (keys.at[pl.ds(0, half_rows), head_columns], heads_x.at[x, y, core, 0]),
        (values.at[pl.ds(0, half_rows), head_columns], heads_x.at[x, y, core, 1]),
        (keys.at[pl.ds(half_rows, half_rows), head_columns], heads_y.at[y, x, core, 0]),
        (values.at[pl.ds(half_rows, half_rows), head_columns], heads_y.at[y, x, core, 1]),
        (queries, q_v),
        (w_gate, own_a.at[pl.ds(0, 64)]),
        (w_down.at[pl.ds(0, 32)], own_a.at[pl.ds(64, 32)]),
        (w_up, own_b.at[pl.ds(0, 64)]),
        (w_down.at[pl.ds(32, 32)], own_b.at[pl.ds(64, 32)]),
        (out_proj, proj_v),
        (resid.at[own_rows], resid_v),
        (gain, gain_v),
        (routes, routes_v),
        (gates, gates_v),
    ]
    local = [pltpu.make_async_copy(src, dst, loads.at[i]) for i, (src, dst) in enumerate(pairs)]
    for copy in local:
        copy.start()

    barrier = pltpu.get_barrier_semaphore()
    neighbours = [to_core] + [{"exp": wrap(place + far, RING)} for far in (1, -1, 2, -2)]
    for far in (1, -1, 2):
        neighbours += [to_x(wrap(x + far, SIDE)), to_y(wrap(y + far, SIDE))]
    for device in neighbours:
        pl.semaphore_signal(barrier, inc=1, device_id=device, device_id_type=MESH)
    pl.semaphore_wait(barrier, len(neighbours))

    x_heads = TorusGather(heads_x, kv_sends.at[0], kv_recvs.at[0], *x_first)
    y_heads = TorusGather(heads_y, kv_sends.at[1], kv_recvs.at[1], *y_first)
    a_gather = TorusGather(abuf, w_sends.at[0], w_recvs.at[0], *x_first)
    b_gather = TorusGather(bbuf, w_sends.at[1], w_recvs.at[1], *y_first)
    heads, experts = (x_heads, y_heads), (a_gather, b_gather)

    for index, gather in enumerate(heads):
        local[2 * index].wait()
        local[2 * index + 1].wait()
        gather.start(0, 1, 2)
    for copy in local[4:]:
        copy.wait()

    all_gates = gates_v[...]
    share = all_gates / jnp.sum(all_gates, axis=0, keepdims=True)
    here = jnp.sum(jnp.where(routes_v[...] == place, share, 0.0), axis=0, keepdims=True)
    weight_v[...] = jnp.broadcast_to(here, (128, TOKENS)).T

    scale = math.log2(math.e) / math.sqrt(HEAD_SIZE)
    key = lax.broadcasted_iota(jnp.int32, (1, BLOCK // 2), 1)
    in_chip = ((key >> 7) & 1) * TOKENS + (key & 127)

    def query_of(part):
        rows = part_rows(q_v[...], part)
        return jnp.concatenate([rows[:, :HEAD_SIZE], rows[:, HEAD_SIZE:]], axis=0).astype(BF16)

    def start_of(part):
        state = (
            jnp.full((2 * half_rows, 1), NEG, F32),
            jnp.zeros((2 * half_rows, 128), F32),
            jnp.zeros((2 * half_rows, HEAD_SIZE), F32),
        )
        return (part, query_of(part), state)

    def visit(task, index):
        part, query, (peak, mass, accum) = task
        at_y, at_x = x_heads.rows[index], y_heads.rows[index]

        def both(kind):
            pieces = (heads_x[:, at_y, :, kind], heads_y[:, at_x, :, kind])
            return jnp.concatenate([piece.reshape(BLOCK // 2, HEAD_SIZE) for piece in pieces], axis=0)

        scores = nt_dot(query, both(0))
        spots = (
            (key >> 8) * (8 * TOKENS) + at_y * (2 * TOKENS) + in_chip,
            (key >> 8) * (2 * TOKENS) + at_x * (8 * TOKENS) + in_chip + half_rows,
        )
        row = lax.broadcasted_iota(jnp.int32, (2 * half_rows, 1), 0) & (half_rows - 1)
        token = (row >> 3) * OWN + (row & (PART - 1)) + part * PART + ctx * TOKENS
        scores = jnp.where(jnp.concatenate(spots, axis=1) <= token, scores, NEG)
        new_peak = jnp.maximum(peak, jnp.max(scores, axis=1, keepdims=True))
        weights = jnp.exp2((scores - new_peak) * scale)
        fade = jnp.exp2((peak - new_peak) * scale)
        some = weights[:, :128]
        for low in range(128, BLOCK, 128):
            some = some + weights[:, low : low + 128]
        mass = mass * fade + some
        accum = accum * fade + dot(weights.astype(BF16), both(1))
        return (part, query, (new_peak, mass, accum))

    def end_of(task):
        _, _, (_, mass, accum) = task
        result = accum / jnp.sum(mass, axis=1, keepdims=True)
        return jnp.concatenate([result[:half_rows], result[half_rows:]], axis=1)

    def project(part, rows):
        halves = [dot(rows.astype(BF16), proj_v[:, low : low + HALF]) for low in (0, HALF)]
        terms[part] = pack(*halves)

    def norm(part):
        total = scatter_one[part].total()
        rows = resid_v[...].astype(F32)[part * PART : (part + 1) * PART]
        hidden = rows + jnp.concatenate([total[:PART], total[PART:]], axis=1)
        spread = lax.rsqrt(jnp.mean(hidden * hidden, axis=1, keepdims=True) + 1e-06)
        own = hidden * spread * gain_v[...]
        normed[part, place] = jnp.concatenate([own[:, :HALF], own[:, HALF:]], axis=0).astype(BF16)
        return hidden

    def expert(part):
        left, right = unpack(normed[part])
        gate_sum = dot(left, abuf[:2, :, :, :64].reshape(HALF, FF))
        gate_sum += dot(right, abuf[2:, :, :, :64].reshape(HALF, FF))
        up_sum = jnp.zeros(gate_sum.shape, F32)
        for quarter in range(SIDE):
            low = quarter % 2 * 512
            some = (left, right)[quarter // 2][:, low : low + 512]
            up_sum += dot(some, bbuf[:, quarter, :, :64].reshape(512, FF))
        act = (gate_sum / (1.0 + jnp.exp(-gate_sum)) * up_sum).astype(BF16)
        weight = part_rows(weight_v[...], part)[:, :1]

        def down(quarter):
            rows = jnp.concatenate([abuf[quarter, :, :, 64:], bbuf[:, quarter, :, 64:]], axis=2)
            some = nt_dot(act, rows.reshape(512, FF)).astype(BF16).astype(F32)
            return jnp.where(weight > 0.0, weight * some, 0.0)

        for low in range(2):
            mixed[part, :, :, low * 512 : low * 512 + 512] = pack(down(low), down(low + 2))

    scatter_one = [RingScatter(terms.at[i], ring_one.at[i], z_sends.at[i], z_recvs.at[i], place) for i in range(2)]
    spread_rows = [RingGather(normed.at[i], z_sends.at[2 + i], z_recvs.at[2 + i], place) for i in range(2)]
    scatter_two = [
        RingScatter(mixed.at[i], ring_two.at[i], z_sends.at[4 + i], z_recvs.at[4 + i], place) for i in range(2)
    ]

    early, late = start_of(0), start_of(1)
    for gather in heads:
        gather.arrive(0, 1, 2)
        gather.start(3, 4, 7)
    for gather in heads:
        gather.arrive(7)
    early = visit(early, 0)
    late = visit(late, 0)
    for gather in heads:
        gather.arrive(3)
        gather.start(5, 8)
        gather.arrive(4)
        gather.start(6, 9)
    for gather in heads:
        gather.arrive(8)
    early = visit(early, 1)
    for gather in heads:
        gather.arrive(9)
    early = visit(early, 2)
    for gather in heads:
        gather.arrive(5, 6)
        gather.start(10)
    for gather in experts:
        gather.start(0, 1, 2)
    for gather in heads:
        gather.arrive(10)
    early = end_of(visit(early, 3))
    project(0, early)
    scatter_one[0].begin()
    late = visit(late, 1)
    late = visit(late, 2)
    late = end_of(visit(late, 3))
    project(1, late)
    scatter_one[1].begin()
    pair = [rows.reshape(RING, PART, 2 * HEAD_SIZE) for rows in (early, late)]
    attn_v[...] = jnp.concatenate(pair, axis=1).reshape(TOKENS, 2 * HEAD_SIZE).astype(BF16)
    attn_copy = pltpu.make_async_copy(attn_v, attn_out, loads.at[len(pairs)])
    attn_copy.start()
    scatter_one[0].relay(3)
    for gather in experts:
        gather.arrive(0, 1, 2)
        gather.start(3, 4, 7)
    scatter_one[1].relay(3)
    for step in (2, 1):
        for part in range(2):
            scatter_one[part].relay(step)
    hidden = []
    for part in range(2):
        hidden.append(norm(part))
        spread_rows[part].send(0)
    for gather in experts:
        gather.arrive(3)
        gather.start(5, 8)
        gather.arrive(4)
        gather.start(6, 9)
    for step in (1, 2, 3):
        for part in range(2):
            spread_rows[part].relay(step)
        if step == 2:
            for gather in experts:
                gather.arrive(5, 6)
                gather.start(10)
    for gather in experts:
        gather.arrive(7, 8, 9, 10)
    for part in range(2):
        spread_rows[part].finish()
        expert(part)
        scatter_two[part].begin()
    attn_copy.wait()
    for gather in (*heads, *experts):
        gather.drain()
    for step in (3, 2, 1):
        for part in range(2):
            scatter_two[part].relay(step)
        if step > 1:
            (scatter_one, spread_rows)[step - 2][0].drain()
            (scatter_one, spread_rows)[step - 2][1].drain()
    done = []
    for part in range(2):
        total = scatter_two[part].total()
        done.append(hidden[part] + jnp.concatenate([total[:PART], total[PART:]], axis=1))
    layer_out[...] = jnp.concatenate(done, axis=0).astype(BF16)
    for part in range(2):
        scatter_two[part].drain()


def local_layer(queries, keys, values, out_proj, resid, norm_gain, routes, gates, w_gate, w_up, w_down):
    anywhere = pl.BlockSpec(memory_space=pl.ANY)
    torus = (SIDE, SIDE, 2)
    pieces = (2, RING, 2 * PART, HALF)
    ring = (2, 2, 2, 4, 2 * PART, HALF)
    ring_sems = pltpu.SemaphoreType.DMA((6, 2, 2, 4))
    gather_sems = pltpu.SemaphoreType.DMA((2, 11))
    return pl.pallas_call(
        layer,
        out_shape=(
            jax.ShapeDtypeStruct(queries.shape, BF16),
            jax.ShapeDtypeStruct((OWN, D), BF16),
        ),
        in_specs=[anywhere] * 11,
        out_specs=(anywhere, pl.BlockSpec(memory_space=pltpu.VMEM)),
        scratch_shapes=[
            pltpu.VMEM((*torus, 2, TOKENS // 2, HEAD_SIZE), BF16),
            pltpu.VMEM((*torus, 2, TOKENS // 2, HEAD_SIZE), BF16),
            pltpu.VMEM((*torus, 96, FF), BF16),
            pltpu.VMEM((*torus, 96, FF), BF16),
            pltpu.VMEM(queries.shape, BF16),
            pltpu.VMEM(out_proj.shape, BF16),
            pltpu.VMEM((OWN, D), BF16),
            pltpu.VMEM((1, D), F32),
            pltpu.VMEM((8, TOKENS), jnp.int32),
            pltpu.VMEM((8, TOKENS), F32),
            pltpu.VMEM((TOKENS, 128), F32),
            pltpu.VMEM(queries.shape, BF16),
            pltpu.VMEM(pieces, BF16),
            pltpu.VMEM(ring, BF16),
            pltpu.VMEM(pieces, BF16),
            pltpu.VMEM(pieces, BF16),
            pltpu.VMEM(ring, BF16),
            pltpu.SemaphoreType.DMA((15,)),
            gather_sems,
            gather_sems,
            gather_sems,
            gather_sems,
            ring_sems,
            ring_sems,
        ],
        compiler_params=pltpu.CompilerParams(
            collective_id=0, has_side_effects=True, vmem_limit_bytes=56 * 1024 * 1024
        ),
        name="layer",
    )(
        queries,
        keys,
        values,
        out_proj,
        resid,
        norm_gain.reshape(1, D),
        routes.T,
        gates.T,
        w_gate[0],
        w_up[0],
        w_down[0].T,
    )


def solution(mesh):
    placed = (
        P("ctx", "exp"),
        P("ctx", None),
        P("ctx", None),
        P("exp", None),
        P("ctx", None),
        P(),
        P("ctx", None),
        P("ctx", None),
        P("exp", "ctx", None),
        P("exp", "ctx", None),
        P("exp", None, "ctx"),
    )
    return jax.shard_map(
        local_layer,
        mesh=mesh,
        in_specs=placed,
        out_specs=(P("ctx", "exp"), P(("ctx", "exp"), None)),
        check_vma=False,
    )
```

```python
import math

import jax
import jax.numpy as jnp
from jax import lax
from jax.experimental import pallas as pl
from jax.experimental.pallas import tpu as pltpu
from jax.sharding import PartitionSpec as P

D = 2048
FF = 768
HEAD_SIZE = 128
KEY_HEAD_SHARERS = 4
SIDE = 4
RING = 16
TOKENS = 256
OWN = 16
HALF = D // 2
PART = OWN // 2
BLOCK = 2048
NEG = -1e30
F32 = jnp.float32
BF16 = jnp.bfloat16
MESH = pl.DeviceIdType.MESH


def wrap(index, size):
    return lax.rem(index + size, jnp.int32(size))


def remote(src, dst, sends, recvs, index, device):
    return pltpu.make_async_remote_copy(
        src_ref=src,
        dst_ref=dst,
        send_sem=sends.at[index],
        recv_sem=recvs.at[index],
        device_id=device,
        device_id_type=MESH,
    )


class TorusGather:
    def __init__(self, buf, sends, recvs, spot, devices):
        first, second, core = spot
        to_first, to_second, to_core = devices
        above, below = wrap(second + 1, SIDE), wrap(second - 1, SIDE)
        self.rows = (second, below, above, wrap(second + 2, SIDE))
        own = buf.at[first, second, core]
        row = buf.at[:, second, core]
        plan = [(own, to_first(wrap(first + far, SIDE))) for far in (1, -1, 2)]
        plan += [
            (row, to_second(above)),
            (row, to_second(below)),
            (buf.at[pl.ds(0, 2), below, core], to_second(above)),
            (buf.at[pl.ds(2, 2), above, core], to_second(below)),
        ]
        plan += [(buf.at[:, other, core], to_core) for other in self.rows]
        self.copies = [
            remote(ref, ref, sends, recvs, index, device) for index, (ref, device) in enumerate(plan)
        ]

    def start(self, *which):
        for index in which:
            self.copies[index].start()

    def arrive(self, *which):
        for index in which:
            self.copies[index].wait_recv()

    def drain(self):
        for copy in self.copies:
            copy.wait_send()


class RingScatter:
    def __init__(self, terms, ring, sends, recvs, place, sign):
        self.terms, self.ring, self.sends, self.recvs, self.place = terms, ring, sends, recvs, place
        self.signs = (sign, -sign)

    def copy(self, way, far, step, src=None):
        dst = self.ring.at[way, far, step]
        device = {"exp": wrap(self.place + self.signs[way] * (1 + far), RING)}
        return remote(dst if src is None else src, dst, self.sends, self.recvs, (way, far, step), device)

    def term(self, way, distance):
        return self.terms.at[wrap(self.place + self.signs[way] * distance, RING)]

    def lend(self, step):
        for way in range(2):
            self.copy(way, 0, step, self.term(way, 2 * step + 1)).start()

    def begin(self):
        self.copy(0, 1, 3, self.term(0, 8)).start()
        self.lend(3)

    def arrived(self, way, step):
        self.copy(way, 0, step).wait_recv()
        total = self.ring[way, 0, step].astype(F32)
        if way == 0 or step < 3:
            self.copy(way, 1, step).wait_recv()
            total += self.ring[way, 1, step].astype(F32)
        return total

    def relay(self, step):
        for way in range(2):
            total = self.arrived(way, step) + self.term(way, 2 * step)[...].astype(F32)
            self.ring[way, 1, step] = total.astype(BF16)
            self.copy(way, 1, step - 1, self.ring.at[way, 1, step]).start()
        self.lend(step - 1)

    def total(self):
        return self.terms[self.place].astype(F32) + self.arrived(0, 0) + self.arrived(1, 0)

    def drain(self):
        for way in range(2):
            for step in range(4):
                self.copy(way, 0, step).wait_send()
                if way == 0 or step < 3:
                    self.copy(way, 1, step).wait_send()


class RingGather:
    def __init__(self, rows, sends, recvs, place, sign):
        self.rows, self.sends, self.recvs, self.place = rows, sends, recvs, place
        self.signs = (sign, -sign)

    def copy(self, way, far, step):
        sign = self.signs[way]
        ref = self.rows.at[wrap(self.place - sign * 2 * step, RING)]
        device = {"exp": wrap(self.place + sign * (1 + far), RING)}
        return remote(ref, ref, self.sends, self.recvs, (way, far, step), device)

    def send(self, step):
        for way in range(2):
            if way == 0 or step < 3:
                self.copy(way, 1, step).start()
        for way in range(2):
            self.copy(way, 0, step).start()

    def relay(self, step):
        for way in range(2):
            self.copy(way, 1, step - 1).wait_recv()
        self.send(step)

    def finish(self):
        for way in range(2):
            for step in range(4):
                self.copy(way, 0, step).wait_recv()
        self.copy(0, 1, 3).wait_recv()

    def drain(self):
        for way in range(2):
            for step in range(4):
                self.copy(way, 0, step).wait_send()
                if way == 0 or step < 3:
                    self.copy(way, 1, step).wait_send()


def pack(left, right):
    parts = [half.reshape(RING, PART, half.shape[1]) for half in (left, right)]
    return jnp.concatenate(parts, axis=1).astype(BF16)


def unpack(pieces):
    wide = pieces.astype(F32)
    width = wide.shape[2]
    return [wide[:, low : low + PART].reshape(RING * PART, width).astype(BF16) for low in (0, PART)]


def part_rows(rows, part):
    wide = rows.astype(F32).reshape(RING, OWN, rows.shape[1])
    return wide[:, part * PART : (part + 1) * PART].reshape(RING * PART, rows.shape[1])


def nt_dot(left, right):
    return lax.dot_general(left, right, (((1,), (1,)), ((), ())), preferred_element_type=F32)


def dot(left, right):
    return jnp.dot(left, right, preferred_element_type=F32)


def layer(
    queries, keys, values, out_proj, resid, gain, routes, gates, w_gate, w_up, w_down,
    attn_out, layer_out,
    heads_x, heads_y, abuf, bbuf, q_v, proj_v, resid_v, gain_v, routes_v, gates_v, weight_v, attn_v,
    terms, ring_one, normed, mixed, ring_two,
    loads, kv_sends, kv_recvs, w_sends, w_recvs, z_sends, z_recvs,
):
    ctx, place = lax.axis_index("ctx"), lax.axis_index("exp")
    x, y, core = lax.div(ctx, 8), lax.rem(lax.div(ctx, 2), 4), lax.rem(ctx, 2)

    def to_x(index):
        return {"ctx": index * 8 + y * 2 + core}

    def to_y(index):
        return {"ctx": x * 8 + index * 2 + core}

    to_core = {"ctx": x * 8 + y * 2 + (1 - core)}
    x_first = ((x, y, core), (to_x, to_y, to_core))
    y_first = ((y, x, core), (to_y, to_x, to_core))

    head_columns = pl.ds(pl.multiple_of(lax.div(place, KEY_HEAD_SHARERS) * HEAD_SIZE, HEAD_SIZE), HEAD_SIZE)
    own_rows = pl.ds(pl.multiple_of(place * OWN, OWN), OWN)
    own_a, own_b = abuf.at[x, y, core], bbuf.at[y, x, core]
    half_rows = RING * PART
    pairs = [
        (keys.at[pl.ds(0, half_rows), head_columns], heads_x.at[x, y, core, 0]),
        (values.at[pl.ds(0, half_rows), head_columns], heads_x.at[x, y, core, 1]),
        (keys.at[pl.ds(half_rows, half_rows), head_columns], heads_y.at[y, x, core, 0]),
        (values.at[pl.ds(half_rows, half_rows), head_columns], heads_y.at[y, x, core, 1]),
        (queries, q_v),
        (w_gate, own_a.at[pl.ds(0, 64)]),
        (w_down.at[pl.ds(0, 32)], own_a.at[pl.ds(64, 32)]),
        (w_up, own_b.at[pl.ds(0, 64)]),
        (w_down.at[pl.ds(32, 32)], own_b.at[pl.ds(64, 32)]),
        (out_proj, proj_v),
        (resid.at[own_rows], resid_v),
        (gain, gain_v),
        (routes, routes_v),
        (gates, gates_v),
    ]
    local = [pltpu.make_async_copy(src, dst, loads.at[i]) for i, (src, dst) in enumerate(pairs)]
    for copy in local:
        copy.start()

    barrier = pltpu.get_barrier_semaphore()
    neighbours = [to_core] + [{"exp": wrap(place + far, RING)} for far in (1, -1, 2, -2)]
    for far in (1, -1, 2):
        neighbours += [to_x(wrap(x + far, SIDE)), to_y(wrap(y + far, SIDE))]
    for device in neighbours:
        pl.semaphore_signal(barrier, inc=1, device_id=device, device_id_type=MESH)
    pl.semaphore_wait(barrier, len(neighbours))

    x_heads = TorusGather(heads_x, kv_sends.at[0], kv_recvs.at[0], *x_first)
    y_heads = TorusGather(heads_y, kv_sends.at[1], kv_recvs.at[1], *y_first)
    a_gather = TorusGather(abuf, w_sends.at[0], w_recvs.at[0], *x_first)
    b_gather = TorusGather(bbuf, w_sends.at[1], w_recvs.at[1], *y_first)
    heads, experts = (x_heads, y_heads), (a_gather, b_gather)

    for index, gather in enumerate(heads):
        local[2 * index].wait()
        local[2 * index + 1].wait()
        gather.start(0, 1, 2)
    for copy in local[4:]:
        copy.wait()

    all_gates = gates_v[...]
    share = all_gates / jnp.sum(all_gates, axis=0, keepdims=True)
    here = jnp.sum(jnp.where(routes_v[...] == place, share, 0.0), axis=0, keepdims=True)
    weight_v[...] = jnp.broadcast_to(here, (128, TOKENS)).T

    scale = math.log2(math.e) / math.sqrt(HEAD_SIZE)
    key = lax.broadcasted_iota(jnp.int32, (1, BLOCK // 2), 1)
    in_chip = ((key >> 7) & 1) * TOKENS + (key & 127)

    def query_of(part):
        rows = part_rows(q_v[...], part)
        return jnp.concatenate([rows[:, :HEAD_SIZE], rows[:, HEAD_SIZE:]], axis=0).astype(BF16)

    def start_of(part):
        state = (
            jnp.full((2 * half_rows, 1), NEG, F32),
            jnp.zeros((2 * half_rows, 128), F32),
            jnp.zeros((2 * half_rows, HEAD_SIZE), F32),
        )
        return (part, query_of(part), state)

    def visit(task, index):
        part, query, (peak, mass, accum) = task
        at_y, at_x = x_heads.rows[index], y_heads.rows[index]

        def both(kind):
            pieces = (heads_x[:, at_y, :, kind], heads_y[:, at_x, :, kind])
            return jnp.concatenate([piece.reshape(BLOCK // 2, HEAD_SIZE) for piece in pieces], axis=0)

        scores = nt_dot(query, both(0))
        spots = (
            (key >> 8) * (8 * TOKENS) + at_y * (2 * TOKENS) + in_chip,
            (key >> 8) * (2 * TOKENS) + at_x * (8 * TOKENS) + in_chip + half_rows,
        )
        row = lax.broadcasted_iota(jnp.int32, (2 * half_rows, 1), 0) & (half_rows - 1)
        token = (row >> 3) * OWN + (row & (PART - 1)) + part * PART + ctx * TOKENS
        scores = jnp.where(jnp.concatenate(spots, axis=1) <= token, scores, NEG)
        new_peak = jnp.maximum(peak, jnp.max(scores, axis=1, keepdims=True))
        weights = jnp.exp2((scores - new_peak) * scale)
        fade = jnp.exp2((peak - new_peak) * scale)
        some = weights[:, :128]
        for low in range(128, BLOCK, 128):
            some = some + weights[:, low : low + 128]
        mass = mass * fade + some
        accum = accum * fade + dot(weights.astype(BF16), both(1))
        return (part, query, (new_peak, mass, accum))

    def end_of(task):
        _, _, (_, mass, accum) = task
        result = accum / jnp.sum(mass, axis=1, keepdims=True)
        return jnp.concatenate([result[:half_rows], result[half_rows:]], axis=1)

    def project(part, rows):
        halves = [dot(rows.astype(BF16), proj_v[:, low : low + HALF]) for low in (0, HALF)]
        terms[part] = pack(*halves)

    def norm(part):
        total = scatter_one[part].total()
        rows = resid_v[...].astype(F32)[part * PART : (part + 1) * PART]
        hidden = rows + jnp.concatenate([total[:PART], total[PART:]], axis=1)
        spread = lax.rsqrt(jnp.mean(hidden * hidden, axis=1, keepdims=True) + 1e-06)
        own = hidden * spread * gain_v[...]
        normed[part, place] = jnp.concatenate([own[:, :HALF], own[:, HALF:]], axis=0).astype(BF16)
        return hidden

    def expert(part):
        left, right = unpack(normed[part])
        gate_sum = dot(left, abuf[:2, :, :, :64].reshape(HALF, FF))
        gate_sum += dot(right, abuf[2:, :, :, :64].reshape(HALF, FF))
        up_sum = jnp.zeros(gate_sum.shape, F32)
        for quarter in range(SIDE):
            low = quarter % 2 * 512
            some = (left, right)[quarter // 2][:, low : low + 512]
            up_sum += dot(some, bbuf[:, quarter, :, :64].reshape(512, FF))
        act = (gate_sum / (1.0 + jnp.exp(-gate_sum)) * up_sum).astype(BF16)
        weight = part_rows(weight_v[...], part)[:, :1]

        def down(quarter):
            rows = jnp.concatenate([abuf[quarter, :, :, 64:], bbuf[:, quarter, :, 64:]], axis=2)
            some = nt_dot(act, rows.reshape(512, FF)).astype(BF16).astype(F32)
            return jnp.where(weight > 0.0, weight * some, 0.0)

        for low in range(2):
            mixed[part, :, :, low * 512 : low * 512 + 512] = pack(down(low), down(low + 2))

    rings = [(z_sends.at[i], z_recvs.at[i], place, 1 - 2 * (i % 2)) for i in range(6)]
    scatter_one = [RingScatter(terms.at[i], ring_one.at[i], *rings[i]) for i in range(2)]
    spread_rows = [RingGather(normed.at[i], *rings[2 + i]) for i in range(2)]
    scatter_two = [RingScatter(mixed.at[i], ring_two.at[i], *rings[4 + i]) for i in range(2)]

    early, late = start_of(0), start_of(1)
    for gather in heads:
        gather.arrive(0, 1, 2)
        gather.start(3, 4, 7)
    for gather in heads:
        gather.arrive(7)
    early = visit(early, 0)
    late = visit(late, 0)
    for gather in heads:
        gather.arrive(3)
        gather.start(5, 8)
        gather.arrive(4)
        gather.start(6, 9)
    for gather in heads:
        gather.arrive(8, 9)
    early = visit(visit(early, 1), 2)
    for gather in heads:
        gather.arrive(5, 6)
        gather.start(10)
    for gather in experts:
        gather.start(0, 1, 2)
    late = visit(late, 1)
    for gather in heads:
        gather.arrive(10)
    early = end_of(visit(early, 3))
    project(0, early)
    scatter_one[0].begin()
    late = end_of(visit(visit(late, 2), 3))
    project(1, late)
    scatter_one[1].begin()
    pair = [rows.reshape(RING, PART, 2 * HEAD_SIZE) for rows in (early, late)]
    attn_v[...] = jnp.concatenate(pair, axis=1).reshape(TOKENS, 2 * HEAD_SIZE).astype(BF16)
    attn_copy = pltpu.make_async_copy(attn_v, attn_out, loads.at[len(pairs)])
    attn_copy.start()
    for gather in experts:
        gather.arrive(0, 1, 2)
        gather.start(3, 4, 7)
    for step in (3, 2, 1):
        for part in range(2):
            scatter_one[part].relay(step)
    hidden = []
    for part in range(2):
        hidden.append(norm(part))
        spread_rows[part].send(0)
    for gather in experts:
        gather.arrive(3)
        gather.start(5, 8)
        gather.arrive(4)
        gather.start(6, 9)
    for step in (1, 2, 3):
        for part in range(2):
            spread_rows[part].relay(step)
        if step == 2:
            for gather in experts:
                gather.arrive(5, 6)
                gather.start(10)
    for gather in experts:
        gather.arrive(7, 8, 9, 10)
    for part in range(2):
        spread_rows[part].finish()
        expert(part)
        scatter_two[part].begin()
    attn_copy.wait()
    for gather in (*heads, *experts):
        gather.drain()
    for step in (3, 2, 1):
        for part in range(2):
            scatter_two[part].relay(step)
        if step > 1:
            (scatter_one, spread_rows)[step - 2][0].drain()
            (scatter_one, spread_rows)[step - 2][1].drain()
    done = []
    for part in range(2):
        total = scatter_two[part].total()
        done.append(hidden[part] + jnp.concatenate([total[:PART], total[PART:]], axis=1))
    layer_out[...] = jnp.concatenate(done, axis=0).astype(BF16)
    for part in range(2):
        scatter_two[part].drain()


def local_layer(queries, keys, values, out_proj, resid, norm_gain, routes, gates, w_gate, w_up, w_down):
    anywhere = pl.BlockSpec(memory_space=pl.ANY)
    torus = (SIDE, SIDE, 2)
    pieces = (2, RING, 2 * PART, HALF)
    ring = (2, 2, 2, 4, 2 * PART, HALF)
    ring_sems = pltpu.SemaphoreType.DMA((6, 2, 2, 4))
    gather_sems = pltpu.SemaphoreType.DMA((2, 11))
    return pl.pallas_call(
        layer,
        out_shape=(
            jax.ShapeDtypeStruct(queries.shape, BF16),
            jax.ShapeDtypeStruct((OWN, D), BF16),
        ),
        in_specs=[anywhere] * 11,
        out_specs=(anywhere, pl.BlockSpec(memory_space=pltpu.VMEM)),
        scratch_shapes=[
            pltpu.VMEM((*torus, 2, TOKENS // 2, HEAD_SIZE), BF16),
            pltpu.VMEM((*torus, 2, TOKENS // 2, HEAD_SIZE), BF16),
            pltpu.VMEM((*torus, 96, FF), BF16),
            pltpu.VMEM((*torus, 96, FF), BF16),
            pltpu.VMEM(queries.shape, BF16),
            pltpu.VMEM(out_proj.shape, BF16),
            pltpu.VMEM((OWN, D), BF16),
            pltpu.VMEM((1, D), F32),
            pltpu.VMEM((8, TOKENS), jnp.int32),
            pltpu.VMEM((8, TOKENS), F32),
            pltpu.VMEM((TOKENS, 128), F32),
            pltpu.VMEM(queries.shape, BF16),
            pltpu.VMEM(pieces, BF16),
            pltpu.VMEM(ring, BF16),
            pltpu.VMEM(pieces, BF16),
            pltpu.VMEM(pieces, BF16),
            pltpu.VMEM(ring, BF16),
            pltpu.SemaphoreType.DMA((15,)),
            gather_sems,
            gather_sems,
            gather_sems,
            gather_sems,
            ring_sems,
            ring_sems,
        ],
        compiler_params=pltpu.CompilerParams(
            collective_id=0, has_side_effects=True, vmem_limit_bytes=56 * 1024 * 1024
        ),
        name="layer",
    )(
        queries,
        keys,
        values,
        out_proj,
        resid,
        norm_gain.reshape(1, D),
        routes.T,
        gates.T,
        w_gate[0],
        w_up[0],
        w_down[0].T,
    )


def solution(mesh):
    placed = (
        P("ctx", "exp"),
        P("ctx", None),
        P("ctx", None),
        P("exp", None),
        P("ctx", None),
        P(),
        P("ctx", None),
        P("ctx", None),
        P("exp", "ctx", None),
        P("exp", "ctx", None),
        P("exp", None, "ctx"),
    )
    return jax.shard_map(
        local_layer,
        mesh=mesh,
        in_specs=placed,
        out_specs=(P("ctx", "exp"), P(("ctx", "exp"), None)),
        check_vma=False,
    )
```

```python
import math

import jax
import jax.numpy as jnp
from jax import lax
from jax.experimental import pallas as pl
from jax.experimental.pallas import tpu as pltpu
from jax.sharding import PartitionSpec as P

D = 2048
FF = 768
HEAD_SIZE = 128
KEY_HEAD_SHARERS = 4
SIDE = 4
RING = 16
TOKENS = 256
OWN = 16
HALF = D // 2
PART = OWN // 2
BLOCK = 2048
NEG = -1e30
F32 = jnp.float32
BF16 = jnp.bfloat16
MESH = pl.DeviceIdType.MESH


def wrap(index, size):
    return lax.rem(index + size, jnp.int32(size))


def remote(src, dst, sends, recvs, index, device):
    return pltpu.make_async_remote_copy(
        src_ref=src,
        dst_ref=dst,
        send_sem=sends.at[index],
        recv_sem=recvs.at[index],
        device_id=device,
        device_id_type=MESH,
    )


class TorusGather:
    def __init__(self, buf, sends, recvs, spot, devices):
        first, second, core = spot
        to_first, to_second, to_core = devices
        above, below = wrap(second + 1, SIDE), wrap(second - 1, SIDE)
        self.rows = (second, below, above, wrap(second + 2, SIDE))
        own = buf.at[first, second, core]
        row = buf.at[:, second, core]
        plan = [(own, to_first(wrap(first + far, SIDE))) for far in (1, -1, 2)]
        plan += [
            (row, to_second(above)),
            (row, to_second(below)),
            (buf.at[pl.ds(0, 2), below, core], to_second(above)),
            (buf.at[pl.ds(2, 2), above, core], to_second(below)),
        ]
        plan += [(buf.at[:, other, core], to_core) for other in self.rows]
        self.copies = [
            remote(ref, ref, sends, recvs, index, device) for index, (ref, device) in enumerate(plan)
        ]

    def start(self, *which):
        for index in which:
            self.copies[index].start()

    def arrive(self, *which):
        for index in which:
            self.copies[index].wait_recv()

    def drain(self):
        for copy in self.copies:
            copy.wait_send()


class RingScatter:
    def __init__(self, terms, ring, sends, recvs, place, sign):
        self.terms, self.ring, self.sends, self.recvs, self.place = terms, ring, sends, recvs, place
        self.signs = (sign, -sign)

    def copy(self, way, far, step, src=None):
        dst = self.ring.at[way, far, step]
        device = {"exp": wrap(self.place + self.signs[way] * (1 + far), RING)}
        return remote(dst if src is None else src, dst, self.sends, self.recvs, (way, far, step), device)

    def term(self, way, distance):
        return self.terms.at[wrap(self.place + self.signs[way] * distance, RING)]

    def lend(self, step):
        for way in range(2):
            self.copy(way, 0, step, self.term(way, 2 * step + 1)).start()

    def begin(self):
        self.copy(0, 1, 3, self.term(0, 8)).start()
        self.lend(3)

    def arrived(self, way, step):
        self.copy(way, 0, step).wait_recv()
        total = self.ring[way, 0, step].astype(F32)
        if way == 0 or step < 3:
            self.copy(way, 1, step).wait_recv()
            total += self.ring[way, 1, step].astype(F32)
        return total

    def relay(self, step):
        self.lend(step - 1)
        for way in range(2):
            total = self.arrived(way, step) + self.term(way, 2 * step)[...].astype(F32)
            self.ring[way, 1, step] = total.astype(BF16)
            self.copy(way, 1, step - 1, self.ring.at[way, 1, step]).start()

    def total(self):
        return self.terms[self.place].astype(F32) + self.arrived(0, 0) + self.arrived(1, 0)

    def drain(self):
        for way in range(2):
            for step in range(4):
                self.copy(way, 0, step).wait_send()
                if way == 0 or step < 3:
                    self.copy(way, 1, step).wait_send()


class RingGather:
    def __init__(self, rows, sends, recvs, place, sign):
        self.rows, self.sends, self.recvs, self.place = rows, sends, recvs, place
        self.signs = (sign, -sign)

    def copy(self, way, far, step):
        sign = self.signs[way]
        ref = self.rows.at[wrap(self.place - sign * 2 * step, RING)]
        device = {"exp": wrap(self.place + sign * (1 + far), RING)}
        return remote(ref, ref, self.sends, self.recvs, (way, far, step), device)

    def send(self, step):
        for way in range(2):
            if way == 0 or step < 3:
                self.copy(way, 1, step).start()
        for way in range(2):
            self.copy(way, 0, step).start()

    def relay(self, step):
        for way in range(2):
            self.copy(way, 1, step - 1).wait_recv()
        self.send(step)

    def finish(self):
        for way in range(2):
            for step in range(4):
                self.copy(way, 0, step).wait_recv()
        self.copy(0, 1, 3).wait_recv()

    def drain(self):
        for way in range(2):
            for step in range(4):
                self.copy(way, 0, step).wait_send()
                if way == 0 or step < 3:
                    self.copy(way, 1, step).wait_send()


def pack(left, right):
    parts = [half.reshape(RING, PART, half.shape[1]) for half in (left, right)]
    return jnp.concatenate(parts, axis=1).astype(BF16)


def unpack(pieces):
    wide = pieces.astype(F32)
    width = wide.shape[2]
    return [wide[:, low : low + PART].reshape(RING * PART, width).astype(BF16) for low in (0, PART)]


def part_rows(rows, part):
    wide = rows.astype(F32).reshape(RING, OWN, rows.shape[1])
    return wide[:, part * PART : (part + 1) * PART].reshape(RING * PART, rows.shape[1])


def nt_dot(left, right):
    return lax.dot_general(left, right, (((1,), (1,)), ((), ())), preferred_element_type=F32)


def dot(left, right):
    return jnp.dot(left, right, preferred_element_type=F32)


def layer(
    queries, keys, values, out_proj, resid, gain, routes, gates, w_gate, w_up, w_down,
    attn_out, layer_out,
    heads_x, heads_y, abuf, bbuf, q_v, proj_v, resid_v, gain_v, routes_v, gates_v, weight_v, attn_v,
    terms, ring_one, normed, mixed, ring_two,
    loads, kv_sends, kv_recvs, w_sends, w_recvs, z_sends, z_recvs,
):
    ctx, place = lax.axis_index("ctx"), lax.axis_index("exp")
    x, y, core = lax.div(ctx, 8), lax.rem(lax.div(ctx, 2), 4), lax.rem(ctx, 2)

    def to_x(index):
        return {"ctx": index * 8 + y * 2 + core}

    def to_y(index):
        return {"ctx": x * 8 + index * 2 + core}

    to_core = {"ctx": x * 8 + y * 2 + (1 - core)}
    x_first = ((x, y, core), (to_x, to_y, to_core))
    y_first = ((y, x, core), (to_y, to_x, to_core))

    head_columns = pl.ds(pl.multiple_of(lax.div(place, KEY_HEAD_SHARERS) * HEAD_SIZE, HEAD_SIZE), HEAD_SIZE)
    own_rows = pl.ds(pl.multiple_of(place * OWN, OWN), OWN)
    own_a, own_b = abuf.at[x, y, core], bbuf.at[y, x, core]
    half_rows = RING * PART
    pairs = [
        (keys.at[pl.ds(0, half_rows), head_columns], heads_x.at[x, y, core, 0]),
        (values.at[pl.ds(0, half_rows), head_columns], heads_x.at[x, y, core, 1]),
        (keys.at[pl.ds(half_rows, half_rows), head_columns], heads_y.at[y, x, core, 0]),
        (values.at[pl.ds(half_rows, half_rows), head_columns], heads_y.at[y, x, core, 1]),
        (queries, q_v),
        (w_gate, own_a.at[pl.ds(0, 64)]),
        (w_down.at[pl.ds(0, 32)], own_a.at[pl.ds(64, 32)]),
        (w_up, own_b.at[pl.ds(0, 64)]),
        (w_down.at[pl.ds(32, 32)], own_b.at[pl.ds(64, 32)]),
        (out_proj, proj_v),
        (resid.at[own_rows], resid_v),
        (gain, gain_v),
        (routes, routes_v),
        (gates, gates_v),
    ]
    local = [pltpu.make_async_copy(src, dst, loads.at[i]) for i, (src, dst) in enumerate(pairs)]
    for copy in local[:4]:
        copy.start()

    barrier = pltpu.get_barrier_semaphore()
    neighbours = [to_core] + [{"exp": wrap(place + far, RING)} for far in (1, -1, 2, -2)]
    for far in (1, -1, 2):
        neighbours += [to_x(wrap(x + far, SIDE)), to_y(wrap(y + far, SIDE))]
    for device in neighbours:
        pl.semaphore_signal(barrier, inc=1, device_id=device, device_id_type=MESH)
    pl.semaphore_wait(barrier, len(neighbours))

    x_heads = TorusGather(heads_x, kv_sends.at[0], kv_recvs.at[0], *x_first)
    y_heads = TorusGather(heads_y, kv_sends.at[1], kv_recvs.at[1], *y_first)
    a_gather = TorusGather(abuf, w_sends.at[0], w_recvs.at[0], *x_first)
    b_gather = TorusGather(bbuf, w_sends.at[1], w_recvs.at[1], *y_first)
    heads, experts = (x_heads, y_heads), (a_gather, b_gather)

    for index, gather in enumerate(heads):
        local[2 * index].wait()
        local[2 * index + 1].wait()
        gather.start(0, 1, 2)
    for copy in local[4:]:
        copy.start()
    for copy in local[4:]:
        copy.wait()

    all_gates = gates_v[...]
    share = all_gates / jnp.sum(all_gates, axis=0, keepdims=True)
    here = jnp.sum(jnp.where(routes_v[...] == place, share, 0.0), axis=0, keepdims=True)
    weight_v[...] = jnp.broadcast_to(here, (128, TOKENS)).T

    scale = math.log2(math.e) / math.sqrt(HEAD_SIZE)
    key = lax.broadcasted_iota(jnp.int32, (1, BLOCK // 2), 1)
    in_chip = ((key >> 7) & 1) * TOKENS + (key & 127)

    def query_of(part):
        rows = part_rows(q_v[...], part)
        return jnp.concatenate([rows[:, :HEAD_SIZE], rows[:, HEAD_SIZE:]], axis=0).astype(BF16)

    def start_of(part):
        state = (
            jnp.full((2 * half_rows, 1), NEG, F32),
            jnp.zeros((2 * half_rows, 128), F32),
            jnp.zeros((2 * half_rows, HEAD_SIZE), F32),
        )
        return (part, query_of(part), state)

    def visit(task, index):
        part, query, (peak, mass, accum) = task
        at_y, at_x = x_heads.rows[index], y_heads.rows[index]

        def both(kind):
            pieces = (heads_x[:, at_y, :, kind], heads_y[:, at_x, :, kind])
            return jnp.concatenate([piece.reshape(BLOCK // 2, HEAD_SIZE) for piece in pieces], axis=0)

        scores = nt_dot(query, both(0))
        spots = (
            (key >> 8) * (8 * TOKENS) + at_y * (2 * TOKENS) + in_chip,
            (key >> 8) * (2 * TOKENS) + at_x * (8 * TOKENS) + in_chip + half_rows,
        )
        row = lax.broadcasted_iota(jnp.int32, (2 * half_rows, 1), 0) & (half_rows - 1)
        token = (row >> 3) * OWN + (row & (PART - 1)) + part * PART + ctx * TOKENS
        scores = jnp.where(jnp.concatenate(spots, axis=1) <= token, scores, NEG)
        new_peak = jnp.maximum(peak, jnp.max(scores, axis=1, keepdims=True))
        weights = jnp.exp2((scores - new_peak) * scale)
        fade = jnp.exp2((peak - new_peak) * scale)
        some = weights[:, :128]
        for low in range(128, BLOCK, 128):
            some = some + weights[:, low : low + 128]
        mass = mass * fade + some
        accum = accum * fade + dot(weights.astype(BF16), both(1))
        return (part, query, (new_peak, mass, accum))

    def end_of(task):
        _, _, (_, mass, accum) = task
        result = accum / jnp.sum(mass, axis=1, keepdims=True)
        return jnp.concatenate([result[:half_rows], result[half_rows:]], axis=1)

    def project(part, rows):
        halves = [dot(rows.astype(BF16), proj_v[:, low : low + HALF]) for low in (0, HALF)]
        terms[part] = pack(*halves)

    def norm(part):
        total = scatter_one[part].total()
        rows = resid_v[...].astype(F32)[part * PART : (part + 1) * PART]
        hidden = rows + jnp.concatenate([total[:PART], total[PART:]], axis=1)
        spread = lax.rsqrt(jnp.mean(hidden * hidden, axis=1, keepdims=True) + 1e-06)
        own = hidden * spread * gain_v[...]
        normed[part, place] = jnp.concatenate([own[:, :HALF], own[:, HALF:]], axis=0).astype(BF16)
        return hidden

    def expert(part):
        left, right = unpack(normed[part])
        gate_sum = dot(left, abuf[:2, :, :, :64].reshape(HALF, FF))
        gate_sum += dot(right, abuf[2:, :, :, :64].reshape(HALF, FF))
        up_sum = jnp.zeros(gate_sum.shape, F32)
        for quarter in range(SIDE):
            low = quarter % 2 * 512
            some = (left, right)[quarter // 2][:, low : low + 512]
            up_sum += dot(some, bbuf[:, quarter, :, :64].reshape(512, FF))
        act = (gate_sum / (1.0 + jnp.exp(-gate_sum)) * up_sum).astype(BF16)
        weight = part_rows(weight_v[...], part)[:, :1]

        def down(quarter):
            rows = jnp.concatenate([abuf[quarter, :, :, 64:], bbuf[:, quarter, :, 64:]], axis=2)
            some = nt_dot(act, rows.reshape(512, FF)).astype(BF16).astype(F32)
            return jnp.where(weight > 0.0, weight * some, 0.0)

        for low in range(2):
            mixed[part, :, :, low * 512 : low * 512 + 512] = pack(down(low), down(low + 2))

    rings = [(z_sends.at[i], z_recvs.at[i], place, 1 - 2 * (i % 2)) for i in range(6)]
    scatter_one = [RingScatter(terms.at[i], ring_one.at[i], *rings[i]) for i in range(2)]
    spread_rows = [RingGather(normed.at[i], *rings[2 + i]) for i in range(2)]
    scatter_two = [RingScatter(mixed.at[i], ring_two.at[i], *rings[4 + i]) for i in range(2)]

    early, late = start_of(0), start_of(1)
    for gather in heads:
        gather.arrive(0, 1, 2)
        gather.start(3, 4, 7)
    for gather in heads:
        gather.arrive(7)
    early = visit(early, 0)
    late = visit(late, 0)
    for gather in heads:
        gather.arrive(3)
        gather.start(5, 8)
        gather.arrive(4)
        gather.start(6, 9)
    for gather in heads:
        gather.arrive(8, 9)
    early = visit(visit(early, 1), 2)
    for gather in heads:
        gather.arrive(5, 6)
        gather.start(10)
    for gather in experts:
        gather.start(0, 1, 2)
    late = visit(late, 1)
    for gather in heads:
        gather.arrive(10)
    early = end_of(visit(early, 3))
    project(0, early)
    scatter_one[0].begin()
    late = end_of(visit(visit(late, 2), 3))
    project(1, late)
    scatter_one[1].begin()
    pair = [rows.reshape(RING, PART, 2 * HEAD_SIZE) for rows in (early, late)]
    attn_v[...] = jnp.concatenate(pair, axis=1).reshape(TOKENS, 2 * HEAD_SIZE).astype(BF16)
    attn_copy = pltpu.make_async_copy(attn_v, attn_out, loads.at[len(pairs)])
    attn_copy.start()
    for gather in experts:
        gather.arrive(0, 1, 2)
        gather.start(3, 4, 7)
    for step in (3, 2, 1):
        for part in range(2):
            scatter_one[part].relay(step)
    hidden = []
    for part in range(2):
        hidden.append(norm(part))
        spread_rows[part].send(0)
    for gather in experts:
        gather.arrive(3)
        gather.start(5, 8)
        gather.arrive(4)
        gather.start(6, 9)
    for step in (1, 2, 3):
        for part in range(2):
            spread_rows[part].relay(step)
        if step == 2:
            for gather in experts:
                gather.arrive(5, 6)
                gather.start(10)
    for gather in experts:
        gather.arrive(7, 8, 9, 10)
    for part in range(2):
        spread_rows[part].finish()
        expert(part)
        scatter_two[part].begin()
    attn_copy.wait()
    for gather in (*heads, *experts):
        gather.drain()
    for step in (3, 2, 1):
        for part in range(2):
            scatter_two[part].relay(step)
        if step > 1:
            (scatter_one, spread_rows)[step - 2][0].drain()
            (scatter_one, spread_rows)[step - 2][1].drain()
    done = []
    for part in range(2):
        total = scatter_two[part].total()
        done.append(hidden[part] + jnp.concatenate([total[:PART], total[PART:]], axis=1))
    layer_out[...] = jnp.concatenate(done, axis=0).astype(BF16)
    for part in range(2):
        scatter_two[part].drain()


def local_layer(queries, keys, values, out_proj, resid, norm_gain, routes, gates, w_gate, w_up, w_down):
    anywhere = pl.BlockSpec(memory_space=pl.ANY)
    torus = (SIDE, SIDE, 2)
    pieces = (2, RING, 2 * PART, HALF)
    ring = (2, 2, 2, 4, 2 * PART, HALF)
    ring_sems = pltpu.SemaphoreType.DMA((6, 2, 2, 4))
    gather_sems = pltpu.SemaphoreType.DMA((2, 11))
    return pl.pallas_call(
        layer,
        out_shape=(
            jax.ShapeDtypeStruct(queries.shape, BF16),
            jax.ShapeDtypeStruct((OWN, D), BF16),
        ),
        in_specs=[anywhere] * 11,
        out_specs=(anywhere, pl.BlockSpec(memory_space=pltpu.VMEM)),
        scratch_shapes=[
            pltpu.VMEM((*torus, 2, TOKENS // 2, HEAD_SIZE), BF16),
            pltpu.VMEM((*torus, 2, TOKENS // 2, HEAD_SIZE), BF16),
            pltpu.VMEM((*torus, 96, FF), BF16),
            pltpu.VMEM((*torus, 96, FF), BF16),
            pltpu.VMEM(queries.shape, BF16),
            pltpu.VMEM(out_proj.shape, BF16),
            pltpu.VMEM((OWN, D), BF16),
            pltpu.VMEM((1, D), F32),
            pltpu.VMEM((8, TOKENS), jnp.int32),
            pltpu.VMEM((8, TOKENS), F32),
            pltpu.VMEM((TOKENS, 128), F32),
            pltpu.VMEM(queries.shape, BF16),
            pltpu.VMEM(pieces, BF16),
            pltpu.VMEM(ring, BF16),
            pltpu.VMEM(pieces, BF16),
            pltpu.VMEM(pieces, BF16),
            pltpu.VMEM(ring, BF16),
            pltpu.SemaphoreType.DMA((15,)),
            gather_sems,
            gather_sems,
            gather_sems,
            gather_sems,
            ring_sems,
            ring_sems,
        ],
        compiler_params=pltpu.CompilerParams(
            collective_id=0, has_side_effects=True, vmem_limit_bytes=56 * 1024 * 1024
        ),
        name="layer",
    )(
        queries,
        keys,
        values,
        out_proj,
        resid,
        norm_gain.reshape(1, D),
        routes.T,
        gates.T,
        w_gate[0],
        w_up[0],
        w_down[0].T,
    )


def solution(mesh):
    placed = (
        P("ctx", "exp"),
        P("ctx", None),
        P("ctx", None),
        P("exp", None),
        P("ctx", None),
        P(),
        P("ctx", None),
        P("ctx", None),
        P("exp", "ctx", None),
        P("exp", "ctx", None),
        P("exp", None, "ctx"),
    )
    return jax.shard_map(
        local_layer,
        mesh=mesh,
        in_specs=placed,
        out_specs=(P("ctx", "exp"), P(("ctx", "exp"), None)),
        check_vma=False,
    )
```
